32 devices in a mesh: models: 2 (over y), gx: 8 (over z, x), gz: 2 (over core).
Axes of the slice: x: 2, y: 2, z: 4, core: 2. Of those that a mesh axis runs over, the one named last changes fastest.
Arguments:
- phases: int32 [32, 128, 512], P(('models', 'gz'), 'gx'), parts along dimension 0, may hold values from 0 to 7
- velocity: float32 [3, 32, 128, 512], P(None, ('models', 'gz'), 'gx'), parts along dimension 1, may hold values from -6 to 6
- pressure: float32 [32, 128, 512], P(('models', 'gz'), 'gx'), parts along dimension 0, may hold values from -6 to 6
- density_table: float32 [8], replicated, may hold values from -4.5 to 4.5
- viscosity_table: float32 [8], replicated, may hold values from 0.5 to 8
Outputs:
- velocity_out: float32 [3, 32, 128, 512], P(None, ('models', 'gz'), 'gx'), parts along dimension 1
- pressure_out: float32 [32, 128, 512], P(('models', 'gz'), 'gx'), parts along dimension 0
- gravity: float32 [256, 512], P(('models', 'gx')), parts along dimension 0
The draws below stay inside these ranges and needn't reach their ends.
There are 2 independent parts, one for each index of `models`. The reference program is written for one: setup_inputs(seed, part) draws one part's arguments, and reference() takes and returns one part's arrays. A program takes and returns all parts, laid end to end along the dimension named above; an argument that names none is the same for every part. Nothing has to cross between parts.
All inputs are finite; a program needn't handle non-finite values.
Results may differ from the reference program's by a relative error of at most 0.00015.
Values sent between devices are 32-bit elements; how exact they have to be, the bound alone decides.
A program may use at most 64 MiB of HBM per device.

```python
import math
import jax
import jax.numpy as jnp
from jax import lax

NY = 512
PHASES = 8
ITERS = 2
NX = 128
NZ = 16


def draw_phases(key, part):
    key = jax.random.fold_in(key, 11)
    column_key, mixing_key, random_key = jax.random.split(key, 3)
    half_count = PHASES // 2
    column_pick = jax.random.randint(column_key, (NX, NY), 0, half_count)
    layer_index = jnp.arange(NZ, dtype=jnp.int32)
    parity = jnp.zeros((NZ,), jnp.int32)
    for bit_place in range(12):
        parity = parity + (layer_index >> bit_place & 1)
    parity = parity % 2
    layered = column_pick[None, :, :] + half_count * parity[:, None, None]
    scatter_mask = jax.random.randint(mixing_key, (NZ, NX, NY), 0, 8) == 0
    random_phase = jax.random.randint(random_key, (NZ, NX, NY), 0, PHASES)
    return jnp.where(scatter_mask, random_phase, layered).astype(jnp.int32)


def draw_density_table(key, part):
    key = jax.random.fold_in(key, 23)
    level_key, mirror_key = jax.random.split(key)
    half_count = PHASES // 2
    levels = 0.3 * jnp.power(2.15, jnp.arange(half_count, dtype=jnp.float32))
    factor = jnp.exp(jax.random.uniform(level_key, (half_count,), jnp.float32, math.log(0.85), math.log(1.15)))
    magnitude = levels * factor
    mirror_ratio = jax.random.uniform(mirror_key, (half_count,), jnp.float32, 0.9, 1.1)
    return jnp.concatenate([magnitude, -magnitude * mirror_ratio]).astype(jnp.float32)


def block_scale(own_key, dims, shards, smallest, top_value):
    factor_of = 1.0
    for position, parts in shards:
        heights = jax.random.uniform(jax.random.fold_in(jax.random.fold_in(own_key, 6), position), (parts,), jnp.float32, smallest / len(shards), top_value / len(shards))
        factor_of = factor_of * jnp.repeat(jnp.exp(heights), dims[position] // parts).reshape((-1,) + (1,) * (len(dims) - 1 - position))
    return factor_of


def normal_values(own_key, shape, scale, bound, cuts=(), kind=jnp.bfloat16):
    gain = block_scale(own_key, shape, cuts, -0.22, 0.18) if cuts else 1.0
    values = jax.random.normal(own_key, shape, jnp.float32) * scale * gain
    return jnp.minimum(jnp.maximum(values, -bound), bound).astype(kind)


def setup_inputs(seed: int = 0, part: int = 0) -> dict:
    splits = jax.random.split(jax.random.key(seed), 6)
    own_keys = jax.random.split(jax.random.fold_in(splits[5], part), 6)
    phases = draw_phases(jax.random.fold_in(jax.random.fold_in(splits[5], part), 71), part)
    velocity = normal_values(own_keys[1], (3, NZ, NX, NY), 1.0, 6.0, ((1, 2), (2, 8)), jnp.float32)
    pressure = normal_values(own_keys[2], (NZ, NX, NY), 1.0, 6.0, ((0, 2), (1, 8)), jnp.float32)
    density_table = draw_density_table(jax.random.fold_in(splits[5], 71), part)
    viscosity_table = jnp.clip(jnp.exp(jax.random.uniform(splits[4], (PHASES,), jnp.float32, math.log(0.5), math.log(8.0))), 0.5, 8.0)
    return {"phases": phases, "velocity": velocity, "pressure": pressure, "density_table": density_table, "viscosity_table": viscosity_table}


velocity_rate = 0.1
pressure_rate = 0.5
bulk_time = 2.0
shear_time = 4.0
squeeze = 0.25
gravity_scale = 4.0
layer_depth = 0.125

def neighbour(field, dim_index, offset):
    lead_count = field.ndim - 3
    pieces = [slice(None)] * lead_count + [slice(1, -1), slice(1, -1), slice(1, -1)]
    pieces[lead_count + dim_index] = slice(2, None) if offset > 0 else slice(0, -2)
    return field[tuple(pieces)]

def center(field):
    lead_count = field.ndim - 3
    pieces = [slice(None)] * lead_count + [slice(1, -1), slice(1, -1), slice(1, -1)]
    return field[tuple(pieces)]

def relaxation(fields, viscous, density, previous):
    padded = jnp.pad(fields, ((0, 0), (0, 0), (0, 0), (1, 1)))
    eta_full = jnp.pad(viscous, ((0, 0), (0, 0), (1, 1)))
    eta_core = center(eta_full)
    pressure_full = padded[3]
    results = []
    for component, dim_index in ((0, 1), (1, 2), (2, 0)):
        moving = padded[component]
        moving_core = center(moving)
        stress = jnp.zeros_like(moving_core)
        for facing in range(3):
            for offset in (1, -1):
                face_eta = 0.5 * (eta_core + neighbour(eta_full, facing, offset))
                stress = stress + face_eta * (neighbour(moving, facing, offset) - moving_core)
        forcing = stress - 0.5 * (neighbour(pressure_full, dim_index, 1) - neighbour(pressure_full, dim_index, -1))
        if component == 2:
            forcing = forcing - density[1:-1, 1:-1, :]
        results.append(moving_core + velocity_rate * forcing / eta_core)
    spread = jnp.zeros_like(eta_core)
    for component, dim_index in ((0, 1), (1, 2), (2, 0)):
        spread = spread + 0.5 * (neighbour(padded[component], dim_index, 1) - neighbour(padded[component], dim_index, -1))
    pressure_core = center(pressure_full)
    results.append(pressure_core - pressure_rate * (spread + (pressure_core - previous[1:-1, 1:-1, :]) / bulk_time))
    return jnp.stack(results)

def centered_wave(index_of, length):
    shifted = jnp.where(index_of < length // 2, index_of, index_of - length)
    return shifted.astype(jnp.float32) * (2.0 * math.pi / length)

def reference(phases, velocity, pressure, density_table, viscosity_table):
    density = density_table[phases]
    viscosity = viscosity_table[phases]
    effective = 1.0 / (1.0 / viscosity + 1.0 / shear_time)
    fields = jnp.concatenate([velocity, pressure[None]], axis=0)
    margin = ((1, 1), (1, 1), (0, 0))
    for sweeps in range(ITERS):
        fields = relaxation(jnp.pad(fields, ((0, 0),) + margin), jnp.pad(effective, margin), jnp.pad(density, margin), jnp.pad(pressure, margin))
    loaded = density * (1.0 + squeeze * fields[3])
    spectrum = jnp.fft.fft2(loaded, axes=(1, 2))
    index_x = jnp.arange(NX, dtype=jnp.int32)
    index_y = jnp.arange(NY, dtype=jnp.int32)
    wave_x = centered_wave(index_x, NX)
    wave_y = centered_wave(index_y, NY)
    magnitude = jnp.sqrt(wave_x[:, None] ** 2 + wave_y[None, :] ** 2)
    depth_of = (jnp.arange(NZ).astype(jnp.float32) + 0.5) * layer_depth
    retained = ((index_y != NY // 2)[None, :] & jnp.logical_not((index_x == 0)[:, None] & (index_y == 0)[None, :])).astype(jnp.float32)
    weights = gravity_scale * layer_depth * jnp.exp(-magnitude[None] * depth_of[:, None, None]) * retained[None]
    summed = lax.optimization_barrier(jnp.sum(weights * spectrum, axis=0))
    gravity = jnp.real(jnp.fft.ifft2(summed)).astype(jnp.float32)
    return (fields[:3], fields[3], gravity)
```

```python
import functools
import math

import jax
import jax.numpy as jnp
import numpy as np
from jax import lax
from jax.experimental import pallas as pl
from jax.experimental.pallas import tpu as pltpu
from jax.sharding import PartitionSpec as P

NY = 512
ITERS = 2


velocity_rate = 0.1
pressure_rate = 0.5
bulk_time = 2.0
shear_time = 4.0
squeeze = 0.25
gravity_scale = 4.0
layer_depth = 0.125
highest = lax.Precision.HIGHEST


def with_halo(block, sides, width):
    for axis, dim in sides:
        count = lax.axis_size(axis)
        forward = [(i, i + 1) for i in range(count - 1)]
        backward = [(target, source) for source, target in forward]
        low = lax.ppermute(
            lax.slice_in_dim(block, block.shape[dim] - width, None, axis=dim), axis, forward
        )
        high = lax.ppermute(lax.slice_in_dim(block, 0, width, axis=dim), axis, backward)
        block = jnp.concatenate([low, block, high], axis=dim)
    return block


def neighbour(field, dim_index, offset):
    lead_count = field.ndim - 3
    pieces = [slice(None)] * lead_count + [slice(1, -1), slice(1, -1), slice(1, -1)]
    pieces[lead_count + dim_index] = slice(2, None) if offset > 0 else slice(0, -2)
    return field[tuple(pieces)]


def center(field):
    lead_count = field.ndim - 3
    pieces = [slice(None)] * lead_count + [slice(1, -1), slice(1, -1), slice(1, -1)]
    return field[tuple(pieces)]


def relaxation(fields, viscous, density, previous):
    padded = jnp.pad(fields, ((0, 0), (0, 0), (0, 0), (1, 1)))
    eta_full = jnp.pad(viscous, ((0, 0), (0, 0), (1, 1)))
    eta_core = center(eta_full)
    pressure_full = padded[3]
    results = []
    for component, dim_index in ((0, 1), (1, 2), (2, 0)):
        moving = padded[component]
        moving_core = center(moving)
        stress = jnp.zeros_like(moving_core)
        for facing in range(3):
            for offset in (1, -1):
                face_eta = 0.5 * (eta_core + neighbour(eta_full, facing, offset))
                stress = stress + face_eta * (neighbour(moving, facing, offset) - moving_core)
        forcing = stress - 0.5 * (
            neighbour(pressure_full, dim_index, 1) - neighbour(pressure_full, dim_index, -1)
        )
        if component == 2:
            forcing = forcing - density[1:-1, 1:-1, :]
        results.append(moving_core + velocity_rate * forcing / eta_core)
    spread = jnp.zeros_like(eta_core)
    for component, dim_index in ((0, 1), (1, 2), (2, 0)):
        spread = spread + 0.5 * (
            neighbour(padded[component], dim_index, 1) - neighbour(padded[component], dim_index, -1)
        )
    pressure_core = center(pressure_full)
    results.append(
        pressure_core
        - pressure_rate * (spread + (pressure_core - previous[1:-1, 1:-1, :]) / bulk_time)
    )
    return jnp.stack(results)


def dft_table(row_count, col_count, period):
    row_index = jnp.arange(row_count, dtype=jnp.int32)[:, None]
    col_index = jnp.arange(col_count, dtype=jnp.int32)[None, :]
    angles = (row_index * col_index % period).astype(jnp.float32) * (2.0 * math.pi / period)
    return (jnp.cos(angles), jnp.sin(angles))


def combine(plain_part, turned, orientation):
    real_part = plain_part[:, :, 0] - orientation * turned[:, :, 1]
    imag_part = plain_part[:, :, 1] + orientation * turned[:, :, 0]
    return jnp.stack([real_part, imag_part], axis=2)


def transform(columns, orientation):
    length = columns.shape[0]
    width_cols = columns.shape[2]
    inner_size = math.gcd(length, 128)
    outer_size = length // inner_size
    blocks = columns.reshape(inner_size, outer_size, 2, width_cols)
    cosine_table, sine_table = dft_table(inner_size, inner_size, inner_size)
    plain_part = jnp.einsum("bajm,bk->kajm", blocks, cosine_table, precision=highest)
    turned = jnp.einsum("bajm,bk->kajm", blocks, sine_table, precision=highest)
    blocks = combine(plain_part, turned, orientation)
    twist_cos, twist_sin = dft_table(inner_size, outer_size, length)
    twist_cos = twist_cos[:, :, None]
    twist_sin = twist_sin[:, :, None]
    real_part = blocks[:, :, 0]
    imag_part = blocks[:, :, 1]
    blocks = jnp.stack(
        [
            real_part * twist_cos - orientation * imag_part * twist_sin,
            imag_part * twist_cos + orientation * real_part * twist_sin,
        ],
        axis=2,
    )
    cosine_table, sine_table = dft_table(outer_size, outer_size, outer_size)
    plain_part = jnp.einsum("kajm,al->lkjm", blocks, cosine_table, precision=highest)
    turned = jnp.einsum("kajm,al->lkjm", blocks, sine_table, precision=highest)
    return combine(plain_part, turned, orientation).reshape(length, 2, width_cols)


def centered_wave(index_of, length):
    shifted = jnp.where(index_of < length // 2, index_of, index_of - length)
    return shifted.astype(jnp.float32) * (2.0 * math.pi / length)


def forward_rows(loaded, mode_count, groups):
    lateral = loaded.shape[2]
    local_modes = mode_count // groups
    cosine_table, sine_table = dft_table(lateral, mode_count, lateral)
    cos_blocks = cosine_table.reshape(lateral, groups, local_modes)
    sin_blocks = sine_table.reshape(lateral, groups, local_modes)
    real_part = jnp.einsum("zxy,ygk->gxzk", loaded, cos_blocks, precision=highest)
    imag_part = -jnp.einsum("zxy,ygk->gxzk", loaded, sin_blocks, precision=highest)
    return jnp.stack([real_part, imag_part], axis=2).reshape(groups, -1)


def fold_depth(received, mode_count, groups, width_cells, depth_cells):
    local_modes = mode_count // groups
    total_x = groups * width_cells
    columns = received.reshape(total_x, 2, depth_cells * local_modes)
    spectrum = transform(columns, -1.0).reshape(total_x, 2, depth_cells, local_modes)
    index_x = jnp.arange(total_x, dtype=jnp.int32)
    index_y = lax.axis_index("gx") * local_modes + jnp.arange(local_modes, dtype=jnp.int32)
    wave_x = centered_wave(index_x, total_x)
    wave_y = centered_wave(index_y, NY)
    magnitude = jnp.sqrt(wave_x[:, None] ** 2 + wave_y[None, :] ** 2)
    depth_of = (
        lax.axis_index("gz") * depth_cells + jnp.arange(depth_cells, dtype=jnp.int32)
    ).astype(jnp.float32)
    depth_of = (depth_of + 0.5) * layer_depth
    retained = (
        (index_y != NY // 2)[None, :]
        & jnp.logical_not((index_x == 0)[:, None] & (index_y == 0)[None, :])
    ).astype(jnp.float32)
    weights = (
        gravity_scale
        * layer_depth
        * jnp.exp(-magnitude[:, None, :] * depth_of[None, :, None])
        * retained[:, None, :]
    )
    partial_value = jnp.sum(weights[:, None] * spectrum, axis=2)
    summed = lax.psum(partial_value, "gz")
    restored = transform(summed, 1.0)
    return restored.reshape(groups, width_cells * 2 * local_modes)


def finish(returned, mode_count, groups, width_cells):
    local_modes = mode_count // groups
    columns = returned.reshape(groups, width_cells, 2, local_modes)
    mode_index = jnp.arange(mode_count, dtype=jnp.int32)
    factor = jnp.where(mode_index == 0, 1.0, 1.0)
    cosine_table, sine_table = dft_table(mode_count, NY, NY)
    cos_blocks = (factor[:, None] * cosine_table).reshape(groups, local_modes, NY)
    sin_blocks = (factor[:, None] * sine_table).reshape(groups, local_modes, NY)
    real_sum = jnp.einsum("sxk,sky->xy", columns[:, :, 0], cos_blocks, precision=highest)
    imag_sum = jnp.einsum("sxk,sky->xy", columns[:, :, 1], sin_blocks, precision=highest)
    return (real_sum - imag_sum) / (groups * width_cells * NY)


def body(phases, velocity, pressure, density_table, viscosity_table):
    classes = jnp.arange(density_table.shape[0], dtype=jnp.int32)[:, None, None, None]
    chosen = phases[None] == classes
    density = jnp.sum(jnp.where(chosen, density_table[:, None, None, None], 0.0), axis=0)
    viscosity = jnp.sum(jnp.where(chosen, viscosity_table[:, None, None, None], 0.0), axis=0)
    effective = 1.0 / (1.0 / viscosity + 1.0 / shear_time)
    depth_cells, width_cells, lateral = pressure.shape
    groups = lax.axis_size("gx")
    fields = jnp.concatenate([velocity, pressure[None]], axis=0)
    margin = ((1, 1), (1, 1), (0, 0))
    for sweeps in range(ITERS):
        stacked = jnp.concatenate([fields, effective[None]], axis=0)
        widened = with_halo(stacked, (("gx", 2), ("gz", 1)), 1)
        fields = relaxation(
            widened[:4], widened[4], jnp.pad(density, margin), jnp.pad(pressure, margin)
        )
    velocity_out = fields[:3]
    pressure_out = fields[3]
    loaded = density * (1.0 + squeeze * pressure_out)
    packed = forward_rows(loaded, lateral, groups)
    received = lax.all_to_all(packed, "gx", split_axis=0, concat_axis=0, tiled=True)
    folded = fold_depth(received, lateral, groups, width_cells, depth_cells)
    returned = lax.all_to_all(folded, "gx", split_axis=0, concat_axis=0, tiled=True)
    gravity = finish(returned, lateral, groups, width_cells)
    return (velocity_out, pressure_out, gravity)


HALF_MODES = NY // 2
MESH = pl.DeviceIdType.MESH


def split_table(table):
    high = table.astype(jnp.bfloat16)
    low = (table - high.astype(np.float32)).astype(jnp.bfloat16)
    return high, low


def host_tables(groups, width, total_x):
    y = np.arange(NY)[:, None]
    k = np.arange(HALF_MODES)[None, :]
    angle = (y * k % NY) * (2.0 * np.pi / NY)
    along_y = np.concatenate([np.cos(angle), -np.sin(angle)], axis=1).astype(np.float32)
    kx = np.arange(total_x)[:, None]
    local = np.arange(width)[None, :]
    angle = (kx * local % total_x) * (2.0 * np.pi / total_x)
    c, s = np.cos(angle), np.sin(angle)
    along_x = np.block([[c, s], [-s, c]]).astype(np.float32)
    high, low = split_table(along_x)
    along_x = np.concatenate([high, high, low], axis=1)
    angle = (kx * np.arange(groups)[None, :] * width % total_x) * (2.0 * np.pi / total_x)
    phase = np.stack([np.cos(angle).T, np.sin(angle).T]).astype(np.float32)
    x = np.arange(total_x)[None, :]
    angle = (kx * x % total_x) * (2.0 * np.pi / total_x)
    c = np.cos(angle).reshape(total_x, groups, 1, width)
    s = np.sin(angle).reshape(total_x, groups, 1, width)
    back_x = np.concatenate(
        [np.concatenate([c, s], axis=2), np.concatenate([-s, c], axis=2)], axis=0
    ).reshape(2 * total_x, groups * 2 * width).astype(np.float32)
    return split_table(along_y), along_x, phase, split_table(back_x)


def split_value(value):
    high = value.astype(jnp.bfloat16)
    low = (value - high.astype(jnp.float32)).astype(jnp.bfloat16)
    return high, low


def dot(left, right):
    return jnp.dot(left, right, preferred_element_type=jnp.float32)


def dot_turned(left, right):
    return lax.dot_general(
        left, right, (((1,), (1,)), ((), ())), preferred_element_type=jnp.float32
    )


def wave_of(index, length):
    shifted = jnp.where(index < length // 2, index, index - length)
    return shifted.astype(jnp.float32) * (2.0 * math.pi / length)


def new_plane(z, src, eta, low, high, eta_low, eta_high, density, inverse, start):
    width, lateral = density.shape[1:]
    row = lax.broadcasted_iota(jnp.int32, (width, lateral), 0)
    lane = lax.broadcasted_iota(jnp.int32, (width, lateral), 1)
    first_row, last_row = row == 0, row == width - 1
    first_lane, last_lane = lane == 0, lane == lateral - 1

    def around(plane, below, above, row_low, row_high):
        return (
            jnp.where(last_row, row_high, pltpu.roll(plane, width - 1, 0)),
            jnp.where(first_row, row_low, pltpu.roll(plane, 1, 0)),
            jnp.where(last_lane, 0.0, pltpu.roll(plane, lateral - 1, 1)),
            jnp.where(first_lane, 0.0, pltpu.roll(plane, 1, 1)),
            above,
            below,
        )

    eta_c = eta(z + 1)
    faces = [
        eta_c + n
        for n in around(eta_c, eta(z), eta(z + 2), eta_low[pl.ds(z, 1), :], eta_high[pl.ds(z, 1), :])
    ]
    total_face = sum(faces[1:], faces[0])
    values, sides = [], []
    for f in range(4):
        plane = src[f, z + 1]
        values.append(plane)
        sides.append(
            around(plane, src[f, z], src[f, z + 2], low[f, pl.ds(z, 1), :], high[f, pl.ds(z, 1), :])
        )
    pressure_sides = sides[3]
    rate = (0.5 * velocity_rate) * inverse[z]
    results = []
    spread = None
    for f in range(3):
        flux = faces[0] * sides[f][0]
        for n in range(1, 6):
            flux = flux + faces[n] * sides[f][n]
        forcing = flux - total_face * values[f]
        forcing = forcing - (pressure_sides[2 * f] - pressure_sides[2 * f + 1])
        if f == 2:
            forcing = forcing - 2.0 * density[z]
        results.append(values[f] + rate * forcing)
        change = sides[f][2 * f] - sides[f][2 * f + 1]
        spread = change if spread is None else spread + change
    results.append(
        values[3]
        - pressure_rate * (0.5 * spread + (values[3] - start(z)) / bulk_time)
    )
    return results


def kernel(
    groups, layers,
    dens_ref, visc_ref, phases_hbm, velocity_hbm, pressure_hbm,
    ty_high_hbm, ty_low_hbm, along_x, phase, bx_high_hbm, bx_low_hbm,
    velocity_out, pressure_out, gravity,
    ph, fields, middle, result, density, inverse,
    send_low, send_high, get_low, get_high, send_low2, send_high2, get_low2, get_high2,
    ty_high, ty_low, bx_high, bx_low,
    loaded, partial, got_z, mine, got_x, back, got_back,
    load_sem, z_sem, x_sem, pair_sem, out_sem, send_sem, recv_sem, send_sem2, recv_sem2,
):
    model, gx, gz = lax.axis_index("models"), lax.axis_index("gx"), lax.axis_index("gz")
    depth, width, lateral = density.shape
    total_x = groups * width
    ranks = groups * layers
    rank = gx * layers + gz

    loads = [
        pltpu.make_async_copy(src, dst, load_sem.at[i])
        for i, (src, dst) in enumerate(
            [
                (phases_hbm, ph),
                (velocity_hbm, fields.at[pl.ds(0, 3), pl.ds(1, depth)]),
                (pressure_hbm, fields.at[3, pl.ds(1, depth)]),
                (ty_high_hbm, ty_high),
                (ty_low_hbm, ty_low),
                (bx_high_hbm, bx_high),
                (bx_low_hbm, bx_low),
            ]
        )
    ]
    for copy in loads:
        copy.start()

    barrier = pltpu.get_barrier_semaphore()
    for j in range(1, ranks):
        other = lax.rem(rank + j, ranks)
        pl.semaphore_signal(
            barrier, inc=1, device_id=(model, other // layers, lax.rem(other, layers)),
            device_id_type=MESH,
        )

    edge = (depth + 1) * gz
    for f in range(5):
        fields[f, edge] = jnp.zeros((width, lateral), jnp.float32)
    for f in range(4):
        middle[f, edge] = jnp.zeros((width, lateral), jnp.float32)

    @pl.when(gx == 0)
    def _():
        get_low[...] = jnp.zeros_like(get_low)
        get_low2[...] = jnp.zeros_like(get_low2)

    @pl.when(gx == groups - 1)
    def _():
        get_high[...] = jnp.zeros_like(get_high)
        get_high2[...] = jnp.zeros_like(get_high2)

    loads[0].wait()

    def look_up(z, carry):
        kind = ph[z]
        dens = jnp.full(kind.shape, dens_ref[0], jnp.float32)
        visc = jnp.full(kind.shape, visc_ref[0], jnp.float32)
        for c in range(1, dens_ref.shape[0]):
            here = kind == c
            dens = jnp.where(here, dens_ref[c], dens)
            visc = jnp.where(here, visc_ref[c], visc)
        inv = 1.0 / visc + 1.0 / shear_time
        density[z] = dens
        inverse[z] = inv
        fields[4, z + 1] = 1.0 / inv
        return carry

    lax.fori_loop(0, depth, look_up, 0)
    loads[1].wait()
    loads[2].wait()

    def exchange(stage, block, count, out_low, out_high, in_low, in_high):
        for f in range(count):
            out_low[f] = block[f, 1 : depth + 1, 0, :]
            out_high[f] = block[f, 1 : depth + 1, width - 1, :]
        across = pltpu.make_async_remote_copy(
            src_ref=block.at[:, depth - (depth - 1) * gz],
            dst_ref=block.at[:, edge],
            send_sem=z_sem.at[2 * stage],
            recv_sem=z_sem.at[2 * stage + 1],
            device_id=(model, gx, 1 - gz),
            device_id_type=MESH,
        )
        downward = pltpu.make_async_remote_copy(
            src_ref=out_low, dst_ref=in_high,
            send_sem=x_sem.at[4 * stage], recv_sem=x_sem.at[4 * stage + 1],
            device_id=(model, lax.rem(gx + groups - 1, groups), gz), device_id_type=MESH,
        )
        upward = pltpu.make_async_remote_copy(
            src_ref=out_high, dst_ref=in_low,
            send_sem=x_sem.at[4 * stage + 2], recv_sem=x_sem.at[4 * stage + 3],
            device_id=(model, lax.rem(gx + 1, groups), gz), device_id_type=MESH,
        )
        if stage == 0:
            pl.semaphore_wait(barrier, ranks - 1)

        @pl.when(gx > 0)
        def _():
            downward.start()

        @pl.when(gx < groups - 1)
        def _():
            upward.start()

        across.start()

        across.wait()

        @pl.when(gx > 0)
        def _():
            downward.wait_send()
            upward.wait_recv()

        @pl.when(gx < groups - 1)
        def _():
            upward.wait_send()
            downward.wait_recv()

    def eta(index):
        return fields[4, index]

    def start(z):
        return fields[3, z + 1]

    eta_low, eta_high = get_low.at[4], get_high.at[4]
    exchange(0, fields, 5, send_low, send_high, get_low, get_high)

    def first(z, carry):
        values = new_plane(
            z, fields, eta, get_low, get_high, eta_low, eta_high, density, inverse, start
        )
        for f in range(4):
            middle[f, z + 1] = values[f]
        return carry

    lax.fori_loop(0, depth, first, 0)
    exchange(1, middle, 4, send_low2, send_high2, get_low2, get_high2)

    def second(z, carry):
        values = new_plane(
            z, middle, eta, get_low2, get_high2, eta_low, eta_high, density, inverse, start
        )
        for f in range(4):
            result[f, z] = values[f]
        loaded[z] = density[z] * (1.0 + squeeze * values[3])
        return carry

    lax.fori_loop(0, depth, second, 0)
    outs = [
        pltpu.make_async_copy(result.at[pl.ds(0, 3)], velocity_out, out_sem.at[0]),
        pltpu.make_async_copy(result.at[3], pressure_out, out_sem.at[1]),
    ]
    for copy in outs:
        copy.start()

    loads[3].wait()
    loads[4].wait()
    high, low = split_value(loaded[...].reshape(depth * width, lateral))
    both = dot(jnp.concatenate([high, low], axis=0), ty_high[...])
    rows = both[: depth * width] + both[depth * width :] + dot(high, ty_low[...])

    index_x = lax.broadcasted_iota(jnp.int32, (total_x, HALF_MODES), 0)
    index_y = lax.broadcasted_iota(jnp.int32, (total_x, HALF_MODES), 1)
    wx, wy = wave_of(index_x, total_x), wave_of(index_y, NY)
    magnitude = jnp.sqrt(wx * wx + wy * wy)
    decay = jnp.exp(-layer_depth * magnitude)
    decay = jnp.concatenate([decay, decay], axis=0)
    weights = along_x[...]
    total = None
    for z in range(depth - 1, -1, -1):
        layer = rows[z * width : (z + 1) * width]
        layer = jnp.concatenate([layer[:, :HALF_MODES], layer[:, HALF_MODES:]], axis=0)
        high, low = split_value(layer)
        spectrum = dot(weights, jnp.concatenate([high, low, high], axis=0))
        total = spectrum if total is None else total * decay + spectrum
    above = jnp.exp(-(layer_depth * depth) * magnitude * gz.astype(jnp.float32))
    real = jnp.transpose(total[:total_x] * above)
    imag = jnp.transpose(total[total_x:] * above)
    cos_row, sin_row = phase[0, pl.ds(gx, 1), :], phase[1, pl.ds(gx, 1), :]
    partial[:, :total_x] = real * cos_row + imag * sin_row
    partial[:, total_x:] = imag * cos_row - real * sin_row

    held = HALF_MODES // layers
    across = pltpu.make_async_remote_copy(
        src_ref=partial.at[pl.ds(pl.multiple_of(held * (1 - gz), held), held)],
        dst_ref=got_z,
        send_sem=pair_sem.at[0], recv_sem=pair_sem.at[1],
        device_id=(model, gx, 1 - gz), device_id_type=MESH,
    )
    across.start()
    across.wait()
    own = held // groups
    mine[...] = partial[pl.ds(pl.multiple_of(held * gz, held), held)] + got_z[...]

    copies = []
    for j in range(1, groups):
        target = lax.rem(gx + j, groups)
        copy = pltpu.make_async_remote_copy(
            src_ref=mine.at[pl.ds(pl.multiple_of(target * own, own), own)],
            dst_ref=got_x.at[gx],
            send_sem=send_sem.at[j], recv_sem=recv_sem.at[j],
            device_id=(model, target, gz), device_id_type=MESH,
        )
        copy.start()
        copies.append(copy)
    index_x = lax.broadcasted_iota(jnp.int32, (own, total_x), 1)
    index_y = lax.broadcasted_iota(jnp.int32, (own, total_x), 0) + (held * gz + own * gx)
    wx, wy = wave_of(index_x, total_x), wave_of(index_y, NY)
    scale = gravity_scale * layer_depth / (total_x * NY)
    weight = scale * jnp.exp((-0.5 * layer_depth) * jnp.sqrt(wx * wx + wy * wy))
    weight = weight * jnp.where(index_y == 0, jnp.where(index_x == 0, 0.0, 1.0), 2.0)
    weight = jnp.concatenate([weight, weight], axis=1)
    summed = mine[pl.ds(pl.multiple_of(gx * own, own), own)]
    for j in range(1, groups):
        copies[j - 1].wait_recv()
        summed = summed + got_x[lax.rem(gx + groups - j, groups)]
    loads[5].wait()
    loads[6].wait()
    high, low = split_value(summed * weight)
    both = dot(jnp.concatenate([high, low], axis=0), bx_high[...])
    columns = both[:own] + both[own:] + dot(high, bx_low[...])
    for part in range(2 * total_x // 128):
        back[part] = columns[:, 128 * part : 128 * (part + 1)]

    per_part = 128 // (2 * width)
    slot = gz * groups + gx
    returns = []
    for j in range(1, ranks):
        other = lax.rem(rank + j, ranks)
        copy = pltpu.make_async_remote_copy(
            src_ref=back.at[(other // layers) // per_part],
            dst_ref=got_back.at[slot],
            send_sem=send_sem2.at[j], recv_sem=recv_sem2.at[j],
            device_id=(model, other // layers, lax.rem(other, layers)), device_id_type=MESH,
        )
        copy.start()
        returns.append(copy)
    got_back[slot] = back[gx // per_part]
    for copy in returns:
        copy.wait_recv()
    waves = got_back[...].reshape(HALF_MODES, 128)
    waves = pltpu.roll(waves, lax.rem(128 - 2 * width * lax.rem(gx, per_part), 128), 1)
    waves = jnp.transpose(waves)
    waves = jnp.concatenate([waves[:width], waves[width : 2 * width]], axis=1)
    high, low = split_value(waves)
    both = dot_turned(jnp.concatenate([high, low], axis=0), ty_high[...])
    gravity[...] = both[:width] + both[width:] + dot_turned(high, ty_low[...])

    for copy in copies + returns:
        copy.wait_send()
    for copy in outs:
        copy.wait()


def fused_body(phases, velocity, pressure, density_table, viscosity_table):
    depth, width, lateral = pressure.shape
    groups, layers = lax.axis_size("gx"), lax.axis_size("gz")
    total_x = groups * width
    ty, along_x, phase, bx = host_tables(groups, width, total_x)
    held = HALF_MODES // layers
    own = held // groups
    ranks = groups * layers
    f32, b16 = jnp.float32, jnp.bfloat16
    vmem = pl.BlockSpec(memory_space=pltpu.VMEM)
    smem = pl.BlockSpec(memory_space=pltpu.SMEM)
    anywhere = pl.BlockSpec(memory_space=pl.ANY)
    rows5, rows4 = pltpu.VMEM((5, depth, lateral), f32), pltpu.VMEM((4, depth, lateral), f32)
    cells = (depth, width, lateral)
    sems = pltpu.SemaphoreType.DMA
    return pl.pallas_call(
        functools.partial(kernel, groups, layers),
        out_shape=(
            jax.ShapeDtypeStruct(velocity.shape, f32),
            jax.ShapeDtypeStruct(pressure.shape, f32),
            jax.ShapeDtypeStruct((width, lateral), f32),
        ),
        in_specs=[smem, smem] + [anywhere] * 5 + [vmem] * 2 + [anywhere] * 2,
        out_specs=(anywhere, anywhere, vmem),
        scratch_shapes=[
            pltpu.VMEM(cells, jnp.int32),
            pltpu.VMEM((5, depth + 2, width, lateral), f32),
            pltpu.VMEM((4, depth + 2, width, lateral), f32),
            pltpu.VMEM((4,) + cells, f32),
            pltpu.VMEM(cells, f32),
            pltpu.VMEM(cells, f32),
            rows5, rows5, rows5, rows5, rows4, rows4, rows4, rows4,
            pltpu.VMEM(ty[0].shape, b16),
            pltpu.VMEM(ty[0].shape, b16),
            pltpu.VMEM(bx[0].shape, b16),
            pltpu.VMEM(bx[0].shape, b16),
            pltpu.VMEM(cells, f32),
            pltpu.VMEM((HALF_MODES, 2 * total_x), f32),
            pltpu.VMEM((held, 2 * total_x), f32),
            pltpu.VMEM((held, 2 * total_x), f32),
            pltpu.VMEM((groups, own, 2 * total_x), f32),
            pltpu.VMEM((2 * total_x // 128, own, 128), f32),
            pltpu.VMEM((ranks, own, 128), f32),
            sems((7,)), sems((4,)), sems((8,)), sems((2,)), sems((2,)),
            sems((groups,)), sems((groups,)), sems((ranks,)), sems((ranks,)),
        ],
        compiler_params=pltpu.CompilerParams(
            collective_id=0, has_side_effects=True, vmem_limit_bytes=40 * 1024 * 1024
        ),
    )(
        density_table, viscosity_table, phases, velocity, pressure,
        jnp.asarray(ty[0]), jnp.asarray(ty[1]), jnp.asarray(along_x), jnp.asarray(phase),
        jnp.asarray(bx[0]), jnp.asarray(bx[1]),
    )


def local_program(phases, velocity, pressure, density_table, viscosity_table):
    depth, width, lateral = pressure.shape
    groups, layers = lax.axis_size("gx"), lax.axis_size("gz")
    fits = layers == 2 and groups * width == 128 and width == 16 and depth % 8 == 0
    chosen = fused_body if fits else body
    return chosen(phases, velocity, pressure, density_table, viscosity_table)


def solution(mesh):
    in_specs = (
        P(("models", "gz"), "gx", None),
        P(None, ("models", "gz"), "gx", None),
        P(("models", "gz"), "gx", None),
        P(),
        P(),
    )
    out_specs = (
        P(None, ("models", "gz"), "gx", None),
        P(("models", "gz"), "gx", None),
        P(("models", "gx"), None),
    )
    return jax.shard_map(local_program, mesh=mesh, in_specs=in_specs, out_specs=out_specs, check_vma=False)
```

```python
import functools
import math

import jax
import jax.numpy as jnp
import numpy as np
from jax import lax
from jax.experimental import pallas as pl
from jax.experimental.pallas import tpu as pltpu
from jax.sharding import PartitionSpec as P

NY = 512
ITERS = 2


velocity_rate = 0.1
pressure_rate = 0.5
bulk_time = 2.0
shear_time = 4.0
squeeze = 0.25
gravity_scale = 4.0
layer_depth = 0.125
highest = lax.Precision.HIGHEST


def with_halo(block, sides, width):
    for axis, dim in sides:
        count = lax.axis_size(axis)
        forward = [(i, i + 1) for i in range(count - 1)]
        backward = [(target, source) for source, target in forward]
        low = lax.ppermute(
            lax.slice_in_dim(block, block.shape[dim] - width, None, axis=dim), axis, forward
        )
        high = lax.ppermute(lax.slice_in_dim(block, 0, width, axis=dim), axis, backward)
        block = jnp.concatenate([low, block, high], axis=dim)
    return block


def neighbour(field, dim_index, offset):
    lead_count = field.ndim - 3
    pieces = [slice(None)] * lead_count + [slice(1, -1), slice(1, -1), slice(1, -1)]
    pieces[lead_count + dim_index] = slice(2, None) if offset > 0 else slice(0, -2)
    return field[tuple(pieces)]


def center(field):
    lead_count = field.ndim - 3
    pieces = [slice(None)] * lead_count + [slice(1, -1), slice(1, -1), slice(1, -1)]
    return field[tuple(pieces)]


def relaxation(fields, viscous, density, previous):
    padded = jnp.pad(fields, ((0, 0), (0, 0), (0, 0), (1, 1)))
    eta_full = jnp.pad(viscous, ((0, 0), (0, 0), (1, 1)))
    eta_core = center(eta_full)
    pressure_full = padded[3]
    results = []
    for component, dim_index in ((0, 1), (1, 2), (2, 0)):
        moving = padded[component]
        moving_core = center(moving)
        stress = jnp.zeros_like(moving_core)
        for facing in range(3):
            for offset in (1, -1):
                face_eta = 0.5 * (eta_core + neighbour(eta_full, facing, offset))
                stress = stress + face_eta * (neighbour(moving, facing, offset) - moving_core)
        forcing = stress - 0.5 * (
            neighbour(pressure_full, dim_index, 1) - neighbour(pressure_full, dim_index, -1)
        )
        if component == 2:
            forcing = forcing - density[1:-1, 1:-1, :]
        results.append(moving_core + velocity_rate * forcing / eta_core)
    spread = jnp.zeros_like(eta_core)
    for component, dim_index in ((0, 1), (1, 2), (2, 0)):
        spread = spread + 0.5 * (
            neighbour(padded[component], dim_index, 1) - neighbour(padded[component], dim_index, -1)
        )
    pressure_core = center(pressure_full)
    results.append(
        pressure_core
        - pressure_rate * (spread + (pressure_core - previous[1:-1, 1:-1, :]) / bulk_time)
    )
    return jnp.stack(results)


def dft_table(row_count, col_count, period):
    row_index = jnp.arange(row_count, dtype=jnp.int32)[:, None]
    col_index = jnp.arange(col_count, dtype=jnp.int32)[None, :]
    angles = (row_index * col_index % period).astype(jnp.float32) * (2.0 * math.pi / period)
    return (jnp.cos(angles), jnp.sin(angles))


def combine(plain_part, turned, orientation):
    real_part = plain_part[:, :, 0] - orientation * turned[:, :, 1]
    imag_part = plain_part[:, :, 1] + orientation * turned[:, :, 0]
    return jnp.stack([real_part, imag_part], axis=2)


def transform(columns, orientation):
    length = columns.shape[0]
    width_cols = columns.shape[2]
    inner_size = math.gcd(length, 128)
    outer_size = length // inner_size
    blocks = columns.reshape(inner_size, outer_size, 2, width_cols)
    cosine_table, sine_table = dft_table(inner_size, inner_size, inner_size)
    plain_part = jnp.einsum("bajm,bk->kajm", blocks, cosine_table, precision=highest)
    turned = jnp.einsum("bajm,bk->kajm", blocks, sine_table, precision=highest)
    blocks = combine(plain_part, turned, orientation)
    twist_cos, twist_sin = dft_table(inner_size, outer_size, length)
    twist_cos = twist_cos[:, :, None]
    twist_sin = twist_sin[:, :, None]
    real_part = blocks[:, :, 0]
    imag_part = blocks[:, :, 1]
    blocks = jnp.stack(
        [
            real_part * twist_cos - orientation * imag_part * twist_sin,
            imag_part * twist_cos + orientation * real_part * twist_sin,
        ],
        axis=2,
    )
    cosine_table, sine_table = dft_table(outer_size, outer_size, outer_size)
    plain_part = jnp.einsum("kajm,al->lkjm", blocks, cosine_table, precision=highest)
    turned = jnp.einsum("kajm,al->lkjm", blocks, sine_table, precision=highest)
    return combine(plain_part, turned, orientation).reshape(length, 2, width_cols)


def centered_wave(index_of, length):
    shifted = jnp.where(index_of < length // 2, index_of, index_of - length)
    return shifted.astype(jnp.float32) * (2.0 * math.pi / length)


def forward_rows(loaded, mode_count, groups):
    lateral = loaded.shape[2]
    local_modes = mode_count // groups
    cosine_table, sine_table = dft_table(lateral, mode_count, lateral)
    cos_blocks = cosine_table.reshape(lateral, groups, local_modes)
    sin_blocks = sine_table.reshape(lateral, groups, local_modes)
    real_part = jnp.einsum("zxy,ygk->gxzk", loaded, cos_blocks, precision=highest)
    imag_part = -jnp.einsum("zxy,ygk->gxzk", loaded, sin_blocks, precision=highest)
    return jnp.stack([real_part, imag_part], axis=2).reshape(groups, -1)


def fold_depth(received, mode_count, groups, width_cells, depth_cells):
    local_modes = mode_count // groups
    total_x = groups * width_cells
    columns = received.reshape(total_x, 2, depth_cells * local_modes)
    spectrum = transform(columns, -1.0).reshape(total_x, 2, depth_cells, local_modes)
    index_x = jnp.arange(total_x, dtype=jnp.int32)
    index_y = lax.axis_index("gx") * local_modes + jnp.arange(local_modes, dtype=jnp.int32)
    wave_x = centered_wave(index_x, total_x)
    wave_y = centered_wave(index_y, NY)
    magnitude = jnp.sqrt(wave_x[:, None] ** 2 + wave_y[None, :] ** 2)
    depth_of = (
        lax.axis_index("gz") * depth_cells + jnp.arange(depth_cells, dtype=jnp.int32)
    ).astype(jnp.float32)
    depth_of = (depth_of + 0.5) * layer_depth
    retained = (
        (index_y != NY // 2)[None, :]
        & jnp.logical_not((index_x == 0)[:, None] & (index_y == 0)[None, :])
    ).astype(jnp.float32)
    weights = (
        gravity_scale
        * layer_depth
        * jnp.exp(-magnitude[:, None, :] * depth_of[None, :, None])
        * retained[:, None, :]
    )
    partial_value = jnp.sum(weights[:, None] * spectrum, axis=2)
    summed = lax.psum(partial_value, "gz")
    restored = transform(summed, 1.0)
    return restored.reshape(groups, width_cells * 2 * local_modes)


def finish(returned, mode_count, groups, width_cells):
    local_modes = mode_count // groups
    columns = returned.reshape(groups, width_cells, 2, local_modes)
    mode_index = jnp.arange(mode_count, dtype=jnp.int32)
    factor = jnp.where(mode_index == 0, 1.0, 1.0)
    cosine_table, sine_table = dft_table(mode_count, NY, NY)
    cos_blocks = (factor[:, None] * cosine_table).reshape(groups, local_modes, NY)
    sin_blocks = (factor[:, None] * sine_table).reshape(groups, local_modes, NY)
    real_sum = jnp.einsum("sxk,sky->xy", columns[:, :, 0], cos_blocks, precision=highest)
    imag_sum = jnp.einsum("sxk,sky->xy", columns[:, :, 1], sin_blocks, precision=highest)
    return (real_sum - imag_sum) / (groups * width_cells * NY)


def body(phases, velocity, pressure, density_table, viscosity_table):
    classes = jnp.arange(density_table.shape[0], dtype=jnp.int32)[:, None, None, None]
    chosen = phases[None] == classes
    density = jnp.sum(jnp.where(chosen, density_table[:, None, None, None], 0.0), axis=0)
    viscosity = jnp.sum(jnp.where(chosen, viscosity_table[:, None, None, None], 0.0), axis=0)
    effective = 1.0 / (1.0 / viscosity + 1.0 / shear_time)
    depth_cells, width_cells, lateral = pressure.shape
    groups = lax.axis_size("gx")
    fields = jnp.concatenate([velocity, pressure[None]], axis=0)
    margin = ((1, 1), (1, 1), (0, 0))
    for sweeps in range(ITERS):
        stacked = jnp.concatenate([fields, effective[None]], axis=0)
        widened = with_halo(stacked, (("gx", 2), ("gz", 1)), 1)
        fields = relaxation(
            widened[:4], widened[4], jnp.pad(density, margin), jnp.pad(pressure, margin)
        )
    velocity_out = fields[:3]
    pressure_out = fields[3]
    loaded = density * (1.0 + squeeze * pressure_out)
    packed = forward_rows(loaded, lateral, groups)
    received = lax.all_to_all(packed, "gx", split_axis=0, concat_axis=0, tiled=True)
    folded = fold_depth(received, lateral, groups, width_cells, depth_cells)
    returned = lax.all_to_all(folded, "gx", split_axis=0, concat_axis=0, tiled=True)
    gravity = finish(returned, lateral, groups, width_cells)
    return (velocity_out, pressure_out, gravity)


HALF_MODES = NY // 2
MESH = pl.DeviceIdType.MESH


def split_table(table):
    high = table.astype(jnp.bfloat16)
    low = (table - high.astype(np.float32)).astype(jnp.bfloat16)
    return high, low


def host_tables(groups, layers, width, total_x):
    y = np.arange(NY)[:, None]
    k = mode_at(np.arange(HALF_MODES), groups * layers)[None, :]
    angle = (y * k % NY) * (2.0 * np.pi / NY)
    along_y = np.concatenate([np.cos(angle), -np.sin(angle)], axis=1).astype(np.float32)
    kx = np.arange(total_x)[:, None]
    local = np.arange(width)[None, :]
    angle = (kx * local % total_x) * (2.0 * np.pi / total_x)
    c, s = np.cos(angle), np.sin(angle)
    along_x = np.block([[c, s], [-s, c]]).astype(np.float32)
    high, low = split_table(along_x)
    along_x = np.concatenate([high, high, low], axis=1)
    angle = (kx * np.arange(groups)[None, :] * width % total_x) * (2.0 * np.pi / total_x)
    phase = np.stack([np.cos(angle).T, np.sin(angle).T]).astype(np.float32)
    x = np.arange(total_x)[None, :]
    angle = (kx * x % total_x) * (2.0 * np.pi / total_x)
    c = np.cos(angle).reshape(total_x, groups, 1, width)
    s = np.sin(angle).reshape(total_x, groups, 1, width)
    back_x = np.concatenate(
        [np.concatenate([c, s], axis=2), np.concatenate([-s, c], axis=2)], axis=0
    ).reshape(2 * total_x, groups * 2 * width).astype(np.float32)
    return np.stack(split_table(along_y)), along_x, phase, np.stack(split_table(back_x))


def mode_at(place, owners):
    return place % (8 * owners) // 8 * 16 + place // (8 * owners) * 8 + place % 8


def split_value(value):
    high = value.astype(jnp.bfloat16)
    low = (value - high.astype(jnp.float32)).astype(jnp.bfloat16)
    return high, low


def dot(left, right):
    return jnp.dot(left, right, preferred_element_type=jnp.float32)


def dot_turned(left, right):
    return lax.dot_general(
        left, right, (((1,), (1,)), ((), ())), preferred_element_type=jnp.float32
    )


def wave_of(index, length):
    shifted = jnp.where(index < length // 2, index, index - length)
    return shifted.astype(jnp.float32) * (2.0 * math.pi / length)


def advance(values, sides, faces, density, inverse, start):
    total_face = sum(faces[1:], faces[0])
    rate = (0.5 * velocity_rate) * inverse
    results = []
    spread = None
    for f in range(3):
        flux = faces[0] * sides[f][0]
        for n in range(1, 6):
            flux = flux + faces[n] * sides[f][n]
        forcing = flux - total_face * values[f]
        forcing = forcing - (sides[3][2 * f] - sides[3][2 * f + 1])
        if f == 2:
            forcing = forcing - 2.0 * density
        results.append(values[f] + rate * forcing)
        change = sides[f][2 * f] - sides[f][2 * f + 1]
        spread = change if spread is None else spread + change
    results.append(
        values[3] - pressure_rate * (0.5 * spread + (values[3] - start) / bulk_time)
    )
    return results


def beside_y(tile):
    lateral = tile.shape[1]
    lane = lax.broadcasted_iota(jnp.int32, tile.shape, 1)
    return (
        jnp.where(lane == lateral - 1, 0.0, pltpu.roll(tile, lateral - 1, 1)),
        jnp.where(lane == 0, 0.0, pltpu.roll(tile, 1, 1)),
    )


def inner_planes(z, block, eta, density, inverse, start):
    def around(ref, lead):
        plane = ref[lead + (z + 1,)]
        width = plane.shape[0]
        ahead, behind = beside_y(plane)
        return plane, (
            pltpu.roll(plane, width - 1, 0), pltpu.roll(plane, 1, 0), ahead, behind,
            ref[lead + (z + 2,)], ref[lead + (z,)],
        )

    center, others = around(eta, ())
    faces = [center + other for other in others]
    pairs = [around(block, (f,)) for f in range(4)]
    return advance(
        [p[0] for p in pairs], [p[1] for p in pairs], faces, density[z], inverse[z], start(z)
    )


def edge_rows(row, block, eta, halo, eta_halo, density, inverse, first):
    depth = density.shape[0]
    inward = 1 if row == 0 else -1

    def around(ref, lead, outer):
        tile = ref[lead + (slice(1, depth + 1), row)]
        layer = lax.broadcasted_iota(jnp.int32, tile.shape, 0)
        below = jnp.where(layer == 0, ref[lead + (slice(0, 1), row)], pltpu.roll(tile, 1, 0))
        above = jnp.where(
            layer == depth - 1,
            ref[lead + (slice(depth + 1, depth + 2), row)],
            pltpu.roll(tile, depth - 1, 0),
        )
        ahead, behind = beside_y(tile)
        inner = ref[lead + (slice(1, depth + 1), row + inward)]
        along = (inner, outer) if row == 0 else (outer, inner)
        return tile, along + (ahead, behind, above, below)

    center, others = around(eta, (), eta_halo[...])
    faces = [center + other for other in others]
    pairs = [around(block, (f,), halo[f]) for f in range(4)]
    return advance(
        [p[0] for p in pairs], [p[1] for p in pairs], faces,
        density[:, row], inverse[:, row], first[3, 1 : depth + 1, row],
    )


def kernel(
    groups, layers,
    dens_ref, visc_ref, phases_hbm, velocity_hbm, pressure_hbm,
    ty_hbm, along_x_hbm, phase_hbm, bx_hbm,
    result, waves_out,
    ph, fields, eta, middle, density, inverse,
    send_low, send_high, get_low, get_high, send_low2, send_high2, get_low2, get_high2,
    eta_send_low, eta_send_high, eta_low, eta_high,
    ty, along_x, phase, bx,
    loaded, partial, got_z, mine, got_x, back, got_back,
    load_sem, z_sem, x_sem, pair_sem, send_sem, recv_sem, send_sem2, recv_sem2,
):
    model, gx, gz = lax.axis_index("models"), lax.axis_index("gx"), lax.axis_index("gz")
    depth, width, lateral = density.shape
    total_x = groups * width
    ranks = groups * layers
    rank = gx * layers + gz
    last = width - 1

    loads = [
        pltpu.make_async_copy(src, dst, load_sem.at[i])
        for i, (src, dst) in enumerate(
            [
                (velocity_hbm, fields.at[pl.ds(0, 3), pl.ds(1, depth)]),
                (pressure_hbm, fields.at[3, pl.ds(1, depth)]),
                (phases_hbm, ph),
                (ty_hbm, ty),
                (along_x_hbm, along_x),
                (phase_hbm, phase),
                (bx_hbm, bx),
            ]
        )
    ]
    for copy in loads:
        copy.start()

    barrier = pltpu.get_barrier_semaphore()
    for j in range(1, ranks):
        other = lax.rem(rank + j, ranks)
        pl.semaphore_signal(
            barrier, inc=1, device_id=(model, other // layers, lax.rem(other, layers)),
            device_id_type=MESH,
        )

    edge = (depth + 1) * gz
    empty = jnp.zeros((width, lateral), jnp.float32)
    eta[edge] = empty
    for f in range(4):
        fields[f, edge] = empty
        middle[f, edge] = empty

    @pl.when(gx == 0)
    def _():
        for ref in (get_low, get_low2, eta_low):
            ref[...] = jnp.zeros_like(ref)

    @pl.when(gx == groups - 1)
    def _():
        for ref in (get_high, get_high2, eta_high):
            ref[...] = jnp.zeros_like(ref)

    def beside_x(stage, out_low, out_high, in_low, in_high):
        down = pltpu.make_async_remote_copy(
            src_ref=out_low, dst_ref=in_high,
            send_sem=x_sem.at[4 * stage], recv_sem=x_sem.at[4 * stage + 1],
            device_id=(model, lax.rem(gx + groups - 1, groups), gz), device_id_type=MESH,
        )
        up = pltpu.make_async_remote_copy(
            src_ref=out_high, dst_ref=in_low,
            send_sem=x_sem.at[4 * stage + 2], recv_sem=x_sem.at[4 * stage + 3],
            device_id=(model, lax.rem(gx + 1, groups), gz), device_id_type=MESH,
        )

        @pl.when(gx > 0)
        def _():
            down.start()

        @pl.when(gx < groups - 1)
        def _():
            up.start()

        return down, up

    def wait_x(pair):
        down, up = pair

        @pl.when(gx > 0)
        def _():
            down.wait_send()
            up.wait_recv()

        @pl.when(gx < groups - 1)
        def _():
            up.wait_send()
            down.wait_recv()

    def beside_z(stage, source, target):
        copy = pltpu.make_async_remote_copy(
            src_ref=source, dst_ref=target,
            send_sem=z_sem.at[2 * stage], recv_sem=z_sem.at[2 * stage + 1],
            device_id=(model, gx, 1 - gz), device_id_type=MESH,
        )
        copy.start()
        return copy

    facing = depth - (depth - 1) * gz
    loads[0].wait()
    loads[1].wait()
    for f in range(4):
        send_low[f] = fields[f, 1 : depth + 1, 0]
        send_high[f] = fields[f, 1 : depth + 1, last]
    pl.semaphore_wait(barrier, ranks - 1)
    x_first = beside_x(0, send_low, send_high, get_low, get_high)
    z_first = beside_z(0, fields.at[:, facing], fields.at[:, edge])

    loads[2].wait()

    def look_up(z, carry):
        kind = ph[z]
        dens = jnp.full(kind.shape, dens_ref[0], jnp.float32)
        visc = jnp.full(kind.shape, visc_ref[0], jnp.float32)
        for c in range(1, dens_ref.shape[0]):
            here = kind == c
            dens = jnp.where(here, dens_ref[c], dens)
            visc = jnp.where(here, visc_ref[c], visc)
        inv = 1.0 / visc + 1.0 / shear_time
        density[z] = dens
        inverse[z] = inv
        eta[z + 1] = 1.0 / inv
        return carry

    lax.fori_loop(0, depth, look_up, 0)
    eta_send_low[...] = eta[1 : depth + 1, 0]
    eta_send_high[...] = eta[1 : depth + 1, last]
    x_eta = beside_x(1, eta_send_low, eta_send_high, eta_low, eta_high)
    z_eta = beside_z(1, eta.at[facing], eta.at[edge])
    z_first.wait()
    z_eta.wait()

    def start(z):
        return fields[3, z + 1]

    def first(z, carry):
        values = inner_planes(z, fields, eta, density, inverse, start)
        for f in range(4):
            middle[f, z + 1] = values[f]
        return carry

    lax.fori_loop(0, depth, first, 0)
    wait_x(x_first)
    wait_x(x_eta)
    for row, halo, eta_halo, out in (
        (0, get_low, eta_low, send_low2), (last, get_high, eta_high, send_high2)
    ):
        values = edge_rows(row, fields, eta, halo, eta_halo, density, inverse, fields)
        for f in range(4):
            out[f] = values[f]
    x_second = beside_x(2, send_low2, send_high2, get_low2, get_high2)
    for f in range(4):
        middle[f, 1 : depth + 1, 0] = send_low2[f]
        middle[f, 1 : depth + 1, last] = send_high2[f]
    beside_z(2, middle.at[:, facing], middle.at[:, edge]).wait()

    def second(z, carry):
        values = inner_planes(z, middle, eta, density, inverse, start)
        for f in range(4):
            result[f, z] = values[f]
        loaded[z] = density[z] * (1.0 + squeeze * values[3])
        return carry

    lax.fori_loop(0, depth, second, 0)

    index_x = lax.broadcasted_iota(jnp.int32, (total_x, HALF_MODES), 0)
    index_y = mode_at(lax.broadcasted_iota(jnp.int32, (total_x, HALF_MODES), 1), ranks)
    wx, wy = wave_of(index_x, total_x), wave_of(index_y, NY)
    magnitude = jnp.sqrt(wx * wx + wy * wy)
    decay = jnp.exp(-layer_depth * magnitude)
    above = jnp.exp(-(layer_depth * depth) * magnitude * gz.astype(jnp.float32))
    for copy in loads[3:]:
        copy.wait()

    wait_x(x_second)
    for row, halo, eta_halo in ((0, get_low2, eta_low), (last, get_high2, eta_high)):
        values = edge_rows(row, middle, eta, halo, eta_halo, density, inverse, fields)
        for f in range(4):
            result[f, :, row] = values[f]
        loaded[:, row] = density[:, row] * (1.0 + squeeze * values[3])

    high, low = split_value(loaded[...].reshape(depth * width, lateral))
    both = dot(jnp.concatenate([high, low], axis=0), ty[0])
    rows = both[: depth * width] + both[depth * width :] + dot(high, ty[1])
    decay = jnp.concatenate([decay, decay], axis=0)
    weights = along_x[...]
    total = None
    for z in range(depth - 1, -1, -1):
        layer = rows[z * width : (z + 1) * width]
        layer = jnp.concatenate([layer[:, :HALF_MODES], layer[:, HALF_MODES:]], axis=0)
        high, low = split_value(layer)
        spectrum = dot(weights, jnp.concatenate([high, low, high], axis=0))
        total = spectrum if total is None else total * decay + spectrum
    real = jnp.transpose(total[:total_x] * above)
    imag = jnp.transpose(total[total_x:] * above)
    cos_row, sin_row = phase[0, pl.ds(gx, 1), :], phase[1, pl.ds(gx, 1), :]
    shape = (2, ranks, 8, total_x)
    partial[:, :, :, :total_x] = (real * cos_row + imag * sin_row).reshape(shape)
    partial[:, :, :, total_x:] = (imag * cos_row - real * sin_row).reshape(shape)

    across = pltpu.make_async_remote_copy(
        src_ref=partial.at[:, pl.ds(groups * (1 - gz), groups)],
        dst_ref=got_z,
        send_sem=pair_sem.at[0], recv_sem=pair_sem.at[1],
        device_id=(model, gx, 1 - gz), device_id_type=MESH,
    )
    across.start()
    across.wait()
    mine[...] = partial[:, pl.ds(groups * gz, groups)] + got_z[...]

    copies = []
    for j in range(1, groups):
        target = lax.rem(gx + j, groups)
        copy = pltpu.make_async_remote_copy(
            src_ref=mine.at[:, target],
            dst_ref=got_x.at[gx],
            send_sem=send_sem.at[j], recv_sem=recv_sem.at[j],
            device_id=(model, target, gz), device_id_type=MESH,
        )
        copy.start()
        copies.append(copy)
    slot = gz * groups + gx
    index_x = lax.broadcasted_iota(jnp.int32, (16, total_x), 1)
    index_y = lax.broadcasted_iota(jnp.int32, (16, total_x), 0) + 16 * slot
    wx, wy = wave_of(index_x, total_x), wave_of(index_y, NY)
    scale = gravity_scale * layer_depth / (total_x * NY)
    weight = scale * jnp.exp((-0.5 * layer_depth) * jnp.sqrt(wx * wx + wy * wy))
    weight = weight * jnp.where(index_y == 0, jnp.where(index_x == 0, 0.0, 1.0), 2.0)
    weight = jnp.concatenate([weight, weight], axis=1)
    summed = mine[:, gx]
    for j in range(1, groups):
        copies[j - 1].wait_recv()
        summed = summed + got_x[lax.rem(gx + groups - j, groups)]
    high, low = split_value(summed.reshape(16, 2 * total_x) * weight)
    both = dot(jnp.concatenate([high, low], axis=0), bx[0])
    columns = both[:16] + both[16:] + dot(high, bx[1])

    lane = lax.broadcasted_iota(jnp.int32, (8, 128), 1)
    span = 2 * width
    for target in range(groups):
        place = span * target
        group, offset = place // 128 * 128, place % 128
        upper = pltpu.roll(columns[:8, group : group + 128], (128 - offset) % 128, 1)
        lower = pltpu.roll(columns[8:, group : group + 128], (128 + span - offset) % 128, 1)
        back[target] = jnp.where(lane < span, upper, lower)
    returns = []
    for j in range(1, ranks):
        other = lax.rem(rank + j, ranks)
        copy = pltpu.make_async_remote_copy(
            src_ref=back.at[other // layers],
            dst_ref=got_back.at[slot],
            send_sem=send_sem2.at[j], recv_sem=recv_sem2.at[j],
            device_id=(model, other // layers, lax.rem(other, layers)), device_id_type=MESH,
        )
        copy.start()
        returns.append(copy)
    got_back[slot] = back[gx]
    for copy in returns:
        copy.wait_recv()
    waves = jnp.transpose(got_back[...].reshape(8 * ranks, 128))
    waves_out[...] = jnp.concatenate(
        [waves[i * width : (i + 1) * width] for i in (0, 2, 1, 3)], axis=1
    )
    for copy in copies + returns:
        copy.wait_send()


def last_kernel(result, waves, ty, velocity_out, pressure_out, gravity, sem):
    outs = [
        pltpu.make_async_copy(result.at[pl.ds(0, 3)], velocity_out, sem.at[0]),
        pltpu.make_async_copy(result.at[3], pressure_out, sem.at[1]),
    ]
    for copy in outs:
        copy.start()
    width = waves.shape[0]
    high, low = split_value(waves[...])
    both = dot_turned(jnp.concatenate([high, low], axis=0), ty[0])
    gravity[...] = both[:width] + both[width:] + dot_turned(high, ty[1])
    for copy in outs:
        copy.wait()


def fused_body(phases, velocity, pressure, density_table, viscosity_table):
    depth, width, lateral = pressure.shape
    groups, layers = lax.axis_size("gx"), lax.axis_size("gz")
    total_x = groups * width
    ty, along_x, phase, bx = host_tables(groups, layers, width, total_x)
    ranks = groups * layers
    f32, b16 = jnp.float32, jnp.bfloat16
    vmem = pl.BlockSpec(memory_space=pltpu.VMEM)
    smem = pl.BlockSpec(memory_space=pltpu.SMEM)
    anywhere = pl.BlockSpec(memory_space=pl.ANY)
    hbm = pl.BlockSpec(memory_space=pltpu.HBM)
    rows = pltpu.VMEM((4, depth, lateral), f32)
    eta_rows = pltpu.VMEM((depth, lateral), f32)
    cells = (depth, width, lateral)
    sems = pltpu.SemaphoreType.DMA
    along_y = jnp.asarray(ty)
    result, waves = pl.pallas_call(
        functools.partial(kernel, groups, layers),
        out_shape=(
            pltpu.VMEM((4,) + cells, f32),
            pltpu.VMEM((width, 2 * HALF_MODES), f32),
        ),
        in_specs=[smem, smem] + [hbm] * 7,
        out_specs=(vmem, vmem),
        scratch_shapes=[
            pltpu.VMEM(cells, jnp.int32),
            pltpu.VMEM((4, depth + 2, width, lateral), f32),
            pltpu.VMEM((depth + 2, width, lateral), f32),
            pltpu.VMEM((4, depth + 2, width, lateral), f32),
            pltpu.VMEM(cells, f32),
            pltpu.VMEM(cells, f32),
            rows, rows, rows, rows, rows, rows, rows, rows,
            eta_rows, eta_rows, eta_rows, eta_rows,
            pltpu.VMEM(ty.shape, b16),
            pltpu.VMEM(along_x.shape, b16),
            pltpu.VMEM(phase.shape, f32),
            pltpu.VMEM(bx.shape, b16),
            pltpu.VMEM(cells, f32),
            pltpu.VMEM((2, ranks, 8, 2 * total_x), f32),
            pltpu.VMEM((2, groups, 8, 2 * total_x), f32),
            pltpu.VMEM((2, groups, 8, 2 * total_x), f32),
            pltpu.VMEM((groups, 2, 8, 2 * total_x), f32),
            pltpu.VMEM((groups, 8, 128), f32),
            pltpu.VMEM((ranks, 8, 128), f32),
            sems((7,)), sems((6,)), sems((12,)), sems((2,)),
            sems((groups,)), sems((groups,)), sems((ranks,)), sems((ranks,)),
        ],
        compiler_params=pltpu.CompilerParams(
            collective_id=0, has_side_effects=True, vmem_limit_bytes=56 * 1024 * 1024
        ),
    )(
        density_table, viscosity_table, phases, velocity, pressure,
        along_y, jnp.asarray(along_x), jnp.asarray(phase), jnp.asarray(bx),
    )
    return pl.pallas_call(
        last_kernel,
        out_shape=(
            jax.ShapeDtypeStruct(velocity.shape, f32),
            jax.ShapeDtypeStruct(pressure.shape, f32),
            jax.ShapeDtypeStruct((width, lateral), f32),
        ),
        in_specs=[vmem] * 3,
        out_specs=(hbm, hbm, vmem),
        scratch_shapes=[sems((2,))],
        compiler_params=pltpu.CompilerParams(vmem_limit_bytes=16 * 1024 * 1024),
    )(result, waves, along_y)


def local_program(phases, velocity, pressure, density_table, viscosity_table):
    depth, width, lateral = pressure.shape
    groups, layers = lax.axis_size("gx"), lax.axis_size("gz")
    fits = layers == 2 and groups * width == 128 and width == 16 and depth % 8 == 0
    chosen = fused_body if fits else body
    return chosen(phases, velocity, pressure, density_table, viscosity_table)


def solution(mesh):
    in_specs = (
        P(("models", "gz"), "gx", None),
        P(None, ("models", "gz"), "gx", None),
        P(("models", "gz"), "gx", None),
        P(),
        P(),
    )
    out_specs = (
        P(None, ("models", "gz"), "gx", None),
        P(("models", "gz"), "gx", None),
        P(("models", "gx"), None),
    )
    return jax.shard_map(local_program, mesh=mesh, in_specs=in_specs, out_specs=out_specs, check_vma=False)
```

```python
import functools
import math

import jax
import jax.numpy as jnp
import numpy as np
from jax import lax
from jax.experimental import pallas as pl
from jax.experimental.pallas import tpu as pltpu
from jax.sharding import PartitionSpec as P

NY = 512
ITERS = 2


velocity_rate = 0.1
pressure_rate = 0.5
bulk_time = 2.0
shear_time = 4.0
squeeze = 0.25
gravity_scale = 4.0
layer_depth = 0.125
highest = lax.Precision.HIGHEST


def with_halo(block, sides, width):
    for axis, dim in sides:
        count = lax.axis_size(axis)
        forward = [(i, i + 1) for i in range(count - 1)]
        backward = [(target, source) for source, target in forward]
        low = lax.ppermute(
            lax.slice_in_dim(block, block.shape[dim] - width, None, axis=dim), axis, forward
        )
        high = lax.ppermute(lax.slice_in_dim(block, 0, width, axis=dim), axis, backward)
        block = jnp.concatenate([low, block, high], axis=dim)
    return block


def neighbour(field, dim_index, offset):
    lead_count = field.ndim - 3
    pieces = [slice(None)] * lead_count + [slice(1, -1), slice(1, -1), slice(1, -1)]
    pieces[lead_count + dim_index] = slice(2, None) if offset > 0 else slice(0, -2)
    return field[tuple(pieces)]


def center(field):
    lead_count = field.ndim - 3
    pieces = [slice(None)] * lead_count + [slice(1, -1), slice(1, -1), slice(1, -1)]
    return field[tuple(pieces)]


def relaxation(fields, viscous, density, previous):
    padded = jnp.pad(fields, ((0, 0), (0, 0), (0, 0), (1, 1)))
    eta_full = jnp.pad(viscous, ((0, 0), (0, 0), (1, 1)))
    eta_core = center(eta_full)
    pressure_full = padded[3]
    results = []
    for component, dim_index in ((0, 1), (1, 2), (2, 0)):
        moving = padded[component]
        moving_core = center(moving)
        stress = jnp.zeros_like(moving_core)
        for facing in range(3):
            for offset in (1, -1):
                face_eta = 0.5 * (eta_core + neighbour(eta_full, facing, offset))
                stress = stress + face_eta * (neighbour(moving, facing, offset) - moving_core)
        forcing = stress - 0.5 * (
            neighbour(pressure_full, dim_index, 1) - neighbour(pressure_full, dim_index, -1)
        )
        if component == 2:
            forcing = forcing - density[1:-1, 1:-1, :]
        results.append(moving_core + velocity_rate * forcing / eta_core)
    spread = jnp.zeros_like(eta_core)
    for component, dim_index in ((0, 1), (1, 2), (2, 0)):
        spread = spread + 0.5 * (
            neighbour(padded[component], dim_index, 1) - neighbour(padded[component], dim_index, -1)
        )
    pressure_core = center(pressure_full)
    results.append(
        pressure_core
        - pressure_rate * (spread + (pressure_core - previous[1:-1, 1:-1, :]) / bulk_time)
    )
    return jnp.stack(results)


def dft_table(row_count, col_count, period):
    row_index = jnp.arange(row_count, dtype=jnp.int32)[:, None]
    col_index = jnp.arange(col_count, dtype=jnp.int32)[None, :]
    angles = (row_index * col_index % period).astype(jnp.float32) * (2.0 * math.pi / period)
    return (jnp.cos(angles), jnp.sin(angles))


def combine(plain_part, turned, orientation):
    real_part = plain_part[:, :, 0] - orientation * turned[:, :, 1]
    imag_part = plain_part[:, :, 1] + orientation * turned[:, :, 0]
    return jnp.stack([real_part, imag_part], axis=2)


def transform(columns, orientation):
    length = columns.shape[0]
    width_cols = columns.shape[2]
    inner_size = math.gcd(length, 128)
    outer_size = length // inner_size
    blocks = columns.reshape(inner_size, outer_size, 2, width_cols)
    cosine_table, sine_table = dft_table(inner_size, inner_size, inner_size)
    plain_part = jnp.einsum("bajm,bk->kajm", blocks, cosine_table, precision=highest)
    turned = jnp.einsum("bajm,bk->kajm", blocks, sine_table, precision=highest)
    blocks = combine(plain_part, turned, orientation)
    twist_cos, twist_sin = dft_table(inner_size, outer_size, length)
    twist_cos = twist_cos[:, :, None]
    twist_sin = twist_sin[:, :, None]
    real_part = blocks[:, :, 0]
    imag_part = blocks[:, :, 1]
    blocks = jnp.stack(
        [
            real_part * twist_cos - orientation * imag_part * twist_sin,
            imag_part * twist_cos + orientation * real_part * twist_sin,
        ],
        axis=2,
    )
    cosine_table, sine_table = dft_table(outer_size, outer_size, outer_size)
    plain_part = jnp.einsum("kajm,al->lkjm", blocks, cosine_table, precision=highest)
    turned = jnp.einsum("kajm,al->lkjm", blocks, sine_table, precision=highest)
    return combine(plain_part, turned, orientation).reshape(length, 2, width_cols)


def centered_wave(index_of, length):
    shifted = jnp.where(index_of < length // 2, index_of, index_of - length)
    return shifted.astype(jnp.float32) * (2.0 * math.pi / length)


def forward_rows(loaded, mode_count, groups):
    lateral = loaded.shape[2]
    local_modes = mode_count // groups
    cosine_table, sine_table = dft_table(lateral, mode_count, lateral)
    cos_blocks = cosine_table.reshape(lateral, groups, local_modes)
    sin_blocks = sine_table.reshape(lateral, groups, local_modes)
    real_part = jnp.einsum("zxy,ygk->gxzk", loaded, cos_blocks, precision=highest)
    imag_part = -jnp.einsum("zxy,ygk->gxzk", loaded, sin_blocks, precision=highest)
    return jnp.stack([real_part, imag_part], axis=2).reshape(groups, -1)


def fold_depth(received, mode_count, groups, width_cells, depth_cells):
    local_modes = mode_count // groups
    total_x = groups * width_cells
    columns = received.reshape(total_x, 2, depth_cells * local_modes)
    spectrum = transform(columns, -1.0).reshape(total_x, 2, depth_cells, local_modes)
    index_x = jnp.arange(total_x, dtype=jnp.int32)
    index_y = lax.axis_index("gx") * local_modes + jnp.arange(local_modes, dtype=jnp.int32)
    wave_x = centered_wave(index_x, total_x)
    wave_y = centered_wave(index_y, NY)
    magnitude = jnp.sqrt(wave_x[:, None] ** 2 + wave_y[None, :] ** 2)
    depth_of = (
        lax.axis_index("gz") * depth_cells + jnp.arange(depth_cells, dtype=jnp.int32)
    ).astype(jnp.float32)
    depth_of = (depth_of + 0.5) * layer_depth
    retained = (
        (index_y != NY // 2)[None, :]
        & jnp.logical_not((index_x == 0)[:, None] & (index_y == 0)[None, :])
    ).astype(jnp.float32)
    weights = (
        gravity_scale
        * layer_depth
        * jnp.exp(-magnitude[:, None, :] * depth_of[None, :, None])
        * retained[:, None, :]
    )
    partial_value = jnp.sum(weights[:, None] * spectrum, axis=2)
    summed = lax.psum(partial_value, "gz")
    restored = transform(summed, 1.0)
    return restored.reshape(groups, width_cells * 2 * local_modes)


def finish(returned, mode_count, groups, width_cells):
    local_modes = mode_count // groups
    columns = returned.reshape(groups, width_cells, 2, local_modes)
    mode_index = jnp.arange(mode_count, dtype=jnp.int32)
    factor = jnp.where(mode_index == 0, 1.0, 1.0)
    cosine_table, sine_table = dft_table(mode_count, NY, NY)
    cos_blocks = (factor[:, None] * cosine_table).reshape(groups, local_modes, NY)
    sin_blocks = (factor[:, None] * sine_table).reshape(groups, local_modes, NY)
    real_sum = jnp.einsum("sxk,sky->xy", columns[:, :, 0], cos_blocks, precision=highest)
    imag_sum = jnp.einsum("sxk,sky->xy", columns[:, :, 1], sin_blocks, precision=highest)
    return (real_sum - imag_sum) / (groups * width_cells * NY)


def body(phases, velocity, pressure, density_table, viscosity_table):
    classes = jnp.arange(density_table.shape[0], dtype=jnp.int32)[:, None, None, None]
    chosen = phases[None] == classes
    density = jnp.sum(jnp.where(chosen, density_table[:, None, None, None], 0.0), axis=0)
    viscosity = jnp.sum(jnp.where(chosen, viscosity_table[:, None, None, None], 0.0), axis=0)
    effective = 1.0 / (1.0 / viscosity + 1.0 / shear_time)
    depth_cells, width_cells, lateral = pressure.shape
    groups = lax.axis_size("gx")
    fields = jnp.concatenate([velocity, pressure[None]], axis=0)
    margin = ((1, 1), (1, 1), (0, 0))
    for sweeps in range(ITERS):
        stacked = jnp.concatenate([fields, effective[None]], axis=0)
        widened = with_halo(stacked, (("gx", 2), ("gz", 1)), 1)
        fields = relaxation(
            widened[:4], widened[4], jnp.pad(density, margin), jnp.pad(pressure, margin)
        )
    velocity_out = fields[:3]
    pressure_out = fields[3]
    loaded = density * (1.0 + squeeze * pressure_out)
    packed = forward_rows(loaded, lateral, groups)
    received = lax.all_to_all(packed, "gx", split_axis=0, concat_axis=0, tiled=True)
    folded = fold_depth(received, lateral, groups, width_cells, depth_cells)
    returned = lax.all_to_all(folded, "gx", split_axis=0, concat_axis=0, tiled=True)
    gravity = finish(returned, lateral, groups, width_cells)
    return (velocity_out, pressure_out, gravity)


HALF_MODES = NY // 2
MESH = pl.DeviceIdType.MESH


def split_table(table):
    high = table.astype(jnp.bfloat16)
    low = (table - high.astype(np.float32)).astype(jnp.bfloat16)
    return high, low


def host_tables(groups, layers, width, total_x):
    y = np.arange(NY)[:, None]
    k = mode_at(np.arange(HALF_MODES), groups * layers)[None, :]
    angle = (y * k % NY) * (2.0 * np.pi / NY)
    along_y = np.concatenate([np.cos(angle), -np.sin(angle)], axis=1).astype(np.float32)
    kx = np.arange(total_x)[:, None]
    local = np.arange(width)[None, :]
    angle = (kx * local % total_x) * (2.0 * np.pi / total_x)
    c, s = np.cos(angle), np.sin(angle)
    along_x = np.block([[c, s], [-s, c]]).astype(np.float32)
    high, low = split_table(along_x)
    along_x = np.concatenate([high, high, low], axis=1)
    angle = (kx * np.arange(groups)[None, :] * width % total_x) * (2.0 * np.pi / total_x)
    phase = np.stack([np.cos(angle).T, np.sin(angle).T]).astype(np.float32)
    x = np.arange(total_x)[None, :]
    angle = (kx * x % total_x) * (2.0 * np.pi / total_x)
    c = np.cos(angle).reshape(total_x, groups, 1, width)
    s = np.sin(angle).reshape(total_x, groups, 1, width)
    back_x = np.concatenate(
        [np.concatenate([c, s], axis=2), np.concatenate([-s, c], axis=2)], axis=0
    ).reshape(2 * total_x, groups * 2 * width).astype(np.float32)
    return np.stack(split_table(along_y)), along_x, phase, np.stack(split_table(back_x))


def mode_at(place, owners):
    return place % (8 * owners) // 8 * 16 + place // (8 * owners) * 8 + place % 8


def split_value(value):
    high = value.astype(jnp.bfloat16)
    low = (value - high.astype(jnp.float32)).astype(jnp.bfloat16)
    return high, low


def dot(left, right):
    return jnp.dot(left, right, preferred_element_type=jnp.float32)


def dot_turned(left, right):
    return lax.dot_general(
        left, right, (((1,), (1,)), ((), ())), preferred_element_type=jnp.float32
    )


def wave_of(index, length):
    shifted = jnp.where(index < length // 2, index, index - length)
    return shifted.astype(jnp.float32) * (2.0 * math.pi / length)


def new_velocity(f, value, side, faces, gradient, density, inverse):
    flux = faces[0] * side[0]
    for n in range(1, 6):
        flux = flux + faces[n] * side[n]
    forcing = flux - sum(faces[1:], faces[0]) * value - gradient
    if f == 2:
        forcing = forcing - 2.0 * density
    return value + (0.5 * velocity_rate) * inverse * forcing


def new_pressure(value, spread, start):
    return value - pressure_rate * (0.5 * spread + (value - start) / bulk_time)


def beside_y(tile):
    lateral = tile.shape[1]
    lane = lax.broadcasted_iota(jnp.int32, tile.shape, 1)
    return (
        jnp.where(lane == lateral - 1, 0.0, pltpu.roll(tile, lateral - 1, 1)),
        jnp.where(lane == 0, 0.0, pltpu.roll(tile, 1, 1)),
    )


def beside_plane(ref, lead, z):
    plane = ref[lead + (z + 1,)]
    width = plane.shape[0]
    ahead, behind = beside_y(plane)
    return plane, (
        pltpu.roll(plane, width - 1, 0), pltpu.roll(plane, 1, 0), ahead, behind,
        ref[lead + (z + 2,)], ref[lead + (z,)],
    )


def inner_velocity(z, block, eta, density, inverse):
    center, others = beside_plane(eta, (), z)
    faces = [center + other for other in others]
    pairs = [beside_plane(block, (f,), z) for f in range(4)]
    push = pairs[3][1]
    return [
        new_velocity(
            f, pairs[f][0], pairs[f][1], faces, push[2 * f] - push[2 * f + 1], density[z], inverse[z]
        )
        for f in range(3)
    ]


def inner_pressure(z, block, start):
    width = block.shape[2]
    along_x, along_y = block[0, z + 1], block[1, z + 1]
    ahead, behind = beside_y(along_y)
    spread = pltpu.roll(along_x, width - 1, 0) - pltpu.roll(along_x, 1, 0)
    spread = spread + (ahead - behind) + (block[2, z + 2] - block[2, z])
    return new_pressure(block[3, z + 1], spread, start[3, z + 1])


def beside_row(ref, lead, row, outer):
    depth = ref.shape[-3] - 2
    tile = ref[lead + (slice(1, depth + 1), row)]
    layer = lax.broadcasted_iota(jnp.int32, tile.shape, 0)
    below = jnp.where(layer == 0, ref[lead + (slice(0, 1), row)], pltpu.roll(tile, 1, 0))
    above = jnp.where(
        layer == depth - 1,
        ref[lead + (slice(depth + 1, depth + 2), row)],
        pltpu.roll(tile, depth - 1, 0),
    )
    ahead, behind = beside_y(tile)
    inner = ref[lead + (slice(1, depth + 1), row + 1 if row == 0 else row - 1)]
    along = (inner, outer) if row == 0 else (outer, inner)
    return tile, along + (ahead, behind, above, below)


def edge_velocity(wanted, row, block, eta, halo, eta_halo, density, inverse):
    center, others = beside_row(eta, (), row, eta_halo[...])
    faces = [center + other for other in others]
    push = beside_row(block, (3,), row, halo[3])[1]
    results = []
    for f in wanted:
        value, side = beside_row(block, (f,), row, halo[f])
        results.append(
            new_velocity(
                f, value, side, faces, push[2 * f] - push[2 * f + 1], density[:, row],
                inverse[:, row],
            )
        )
    return results


def edge_pressure(row, block, halo, start):
    depth = block.shape[1] - 2
    spread = None
    for f in range(3):
        side = beside_row(block, (f,), row, halo[f])[1]
        change = side[2 * f] - side[2 * f + 1]
        spread = change if spread is None else spread + change
    here = slice(1, depth + 1)
    return new_pressure(block[3, here, row], spread, start[3, here, row])


def kernel(
    groups, layers,
    dens_ref, visc_ref, phases_hbm, velocity_hbm, pressure_hbm,
    ty_hbm, along_x_hbm, phase_hbm, bx_hbm,
    result, waves_out,
    ph, fields, eta, middle, density, inverse,
    send_low, send_high, get_low, get_high, send_low2, send_high2, get_low2, get_high2,
    eta_send_low, eta_send_high, eta_low, eta_high,
    ty, along_x, phase, bx,
    loaded, partial, got_z, mine, got_x, back, got_back,
    load_sem, z_sem, x_sem, pair_sem, send_sem, recv_sem, send_sem2, recv_sem2,
):
    model, gx, gz = lax.axis_index("models"), lax.axis_index("gx"), lax.axis_index("gz")
    depth, width, lateral = density.shape
    total_x = groups * width
    ranks = groups * layers
    rank = gx * layers + gz
    last = width - 1

    loads = [
        pltpu.make_async_copy(src, dst, load_sem.at[i])
        for i, (src, dst) in enumerate(
            [
                (velocity_hbm, fields.at[pl.ds(0, 3), pl.ds(1, depth)]),
                (pressure_hbm, fields.at[3, pl.ds(1, depth)]),
                (phases_hbm, ph),
                (ty_hbm, ty),
                (along_x_hbm, along_x),
                (phase_hbm, phase),
                (bx_hbm, bx),
            ]
        )
    ]
    for copy in loads[:3]:
        copy.start()

    barrier = pltpu.get_barrier_semaphore()
    for j in range(1, ranks):
        other = lax.rem(rank + j, ranks)
        pl.semaphore_signal(
            barrier, inc=1, device_id=(model, other // layers, lax.rem(other, layers)),
            device_id_type=MESH,
        )

    edge = (depth + 1) * gz
    empty = jnp.zeros((width, lateral), jnp.float32)
    eta[edge] = empty
    for f in range(4):
        fields[f, edge] = empty
        middle[f, edge] = empty

    @pl.when(gx == 0)
    def _():
        for ref in (get_low, get_low2, eta_low):
            ref[...] = jnp.zeros_like(ref)

    @pl.when(gx == groups - 1)
    def _():
        for ref in (get_high, get_high2, eta_high):
            ref[...] = jnp.zeros_like(ref)

    def beside_x(stage, out_low, out_high, in_low, in_high):
        down = pltpu.make_async_remote_copy(
            src_ref=out_low, dst_ref=in_high,
            send_sem=x_sem.at[4 * stage], recv_sem=x_sem.at[4 * stage + 1],
            device_id=(model, lax.rem(gx + groups - 1, groups), gz), device_id_type=MESH,
        )
        up = pltpu.make_async_remote_copy(
            src_ref=out_high, dst_ref=in_low,
            send_sem=x_sem.at[4 * stage + 2], recv_sem=x_sem.at[4 * stage + 3],
            device_id=(model, lax.rem(gx + 1, groups), gz), device_id_type=MESH,
        )
        return down, up

    def send(pairs, rows=(0, last)):
        if 0 in rows:
            @pl.when(gx > 0)
            def _():
                for down, up in pairs:
                    down.start()

        if last in rows:
            @pl.when(gx < groups - 1)
            def _():
                for down, up in pairs:
                    up.start()

    def receive(pairs, row):
        if row == 0:
            @pl.when(gx > 0)
            def _():
                for down, up in pairs:
                    up.wait_recv()
        else:
            @pl.when(gx < groups - 1)
            def _():
                for down, up in pairs:
                    down.wait_recv()

    def all_sent(pairs):
        @pl.when(gx > 0)
        def _():
            for down, up in pairs:
                down.wait_send()

        @pl.when(gx < groups - 1)
        def _():
            for down, up in pairs:
                up.wait_send()

    def beside_z(stage, source, target):
        copy = pltpu.make_async_remote_copy(
            src_ref=source, dst_ref=target,
            send_sem=z_sem.at[2 * stage], recv_sem=z_sem.at[2 * stage + 1],
            device_id=(model, gx, 1 - gz), device_id_type=MESH,
        )
        copy.start()
        return copy

    bundle = (send_low, send_high, get_low, get_high)
    bundle2 = (send_low2, send_high2, get_low2, get_high2)
    x_u = beside_x(0, *[ref.at[0] for ref in bundle])
    x_p = beside_x(1, *[ref.at[3] for ref in bundle])
    x_eta = beside_x(2, eta_send_low, eta_send_high, eta_low, eta_high)
    x_rest = beside_x(3, *[ref.at[pl.ds(1, 2)] for ref in bundle])
    x_u2 = beside_x(4, *[ref.at[0] for ref in bundle2])
    x_rest2 = beside_x(5, *[ref.at[pl.ds(1, 3)] for ref in bundle2])
    edges = (
        (0, get_low, eta_low, send_low2, get_low2),
        (last, get_high, eta_high, send_high2, get_high2),
    )

    facing = depth - (depth - 1) * gz
    loads[0].wait()
    loads[1].wait()
    for f in range(4):
        send_low[f] = fields[f, 1 : depth + 1, 0]
        send_high[f] = fields[f, 1 : depth + 1, last]
    pl.semaphore_wait(barrier, ranks - 1)
    send([x_u, x_p])
    z_first = beside_z(0, fields.at[:, facing], fields.at[:, edge])

    loads[2].wait()
    for copy in loads[3:]:
        copy.start()

    def look_up(z, carry):
        kind = ph[z]
        dens = jnp.full(kind.shape, dens_ref[0], jnp.float32)
        visc = jnp.full(kind.shape, visc_ref[0], jnp.float32)
        for c in range(1, dens_ref.shape[0]):
            here = kind == c
            dens = jnp.where(here, dens_ref[c], dens)
            visc = jnp.where(here, visc_ref[c], visc)
        inv = 1.0 / visc + 1.0 / shear_time
        density[z] = dens
        inverse[z] = inv
        eta[z + 1] = 1.0 / inv
        return carry

    lax.fori_loop(0, depth, look_up, 0)
    eta_send_low[...] = eta[1 : depth + 1, 0]
    eta_send_high[...] = eta[1 : depth + 1, last]
    send([x_eta, x_rest])
    z_eta = beside_z(1, eta.at[facing], eta.at[edge])
    z_first.wait()
    z_eta.wait()

    def first(z, carry):
        values = inner_velocity(z, fields, eta, density, inverse)
        for f in range(3):
            middle[f, z + 1] = values[f]
        middle[3, z + 1] = inner_pressure(z, fields, fields)
        return carry

    lax.fori_loop(0, depth, first, 0)

    for row, halo, eta_halo, out, later in edges:
        receive([x_u, x_p, x_eta], row)
        out[0] = edge_velocity((0,), row, fields, eta, halo, eta_halo, density, inverse)[0]
        send([x_u2], (row,))
    for row, halo, eta_halo, out, later in edges:
        receive([x_rest], row)
        out[1], out[2] = edge_velocity(
            (1, 2), row, fields, eta, halo, eta_halo, density, inverse
        )
        out[3] = edge_pressure(row, fields, halo, fields)
    for row, halo, eta_halo, out, later in edges:
        for f in range(4):
            middle[f, 1 : depth + 1, row] = out[f]
    z_second = beside_z(2, middle.at[:, facing], middle.at[:, edge])
    send([x_rest2])
    z_second.wait()

    def second(z, carry):
        pressure = inner_pressure(z, middle, fields)
        result[3, z] = pressure
        loaded[z] = density[z] * (1.0 + squeeze * pressure)
        return carry

    lax.fori_loop(0, depth, second, 0)

    index_x = lax.broadcasted_iota(jnp.int32, (total_x, HALF_MODES), 0)
    index_y = mode_at(lax.broadcasted_iota(jnp.int32, (total_x, HALF_MODES), 1), ranks)
    wx, wy = wave_of(index_x, total_x), wave_of(index_y, NY)
    magnitude = jnp.sqrt(wx * wx + wy * wy)
    decay = jnp.exp(-layer_depth * magnitude)
    above = jnp.exp(-(layer_depth * depth) * magnitude * gz.astype(jnp.float32))
    for copy in loads[3:]:
        copy.wait()
    for row, halo, eta_halo, out, later in edges:
        receive([x_u2], row)
        pressure = edge_pressure(row, middle, later, fields)
        result[3, :, row] = pressure
        loaded[:, row] = density[:, row] * (1.0 + squeeze * pressure)

    high, low = split_value(loaded[...].reshape(depth * width, lateral))
    both = dot(jnp.concatenate([high, low], axis=0), ty[0])
    rows = both[: depth * width] + both[depth * width :] + dot(high, ty[1])
    decay = jnp.concatenate([decay, decay], axis=0)
    weights = along_x[...]
    total = None
    for z in range(depth - 1, -1, -1):
        layer = rows[z * width : (z + 1) * width]
        layer = jnp.concatenate([layer[:, :HALF_MODES], layer[:, HALF_MODES:]], axis=0)
        high, low = split_value(layer)
        spectrum = dot(weights, jnp.concatenate([high, low, high], axis=0))
        total = spectrum if total is None else total * decay + spectrum
    real = jnp.transpose(total[:total_x] * above)
    imag = jnp.transpose(total[total_x:] * above)
    cos_row, sin_row = phase[0, pl.ds(gx, 1), :], phase[1, pl.ds(gx, 1), :]
    shape = (2, ranks, 8, total_x)
    partial[:, :, :, :total_x] = (real * cos_row + imag * sin_row).reshape(shape)
    partial[:, :, :, total_x:] = (imag * cos_row - real * sin_row).reshape(shape)

    across = pltpu.make_async_remote_copy(
        src_ref=partial.at[:, pl.ds(groups * (1 - gz), groups)],
        dst_ref=got_z,
        send_sem=pair_sem.at[0], recv_sem=pair_sem.at[1],
        device_id=(model, gx, 1 - gz), device_id_type=MESH,
    )
    across.start()
    across.wait()
    mine[...] = partial[:, pl.ds(groups * gz, groups)] + got_z[...]

    copies = []
    distant = sorted(range(1, groups), key=lambda j: -min(j, groups - j))
    for j in distant:
        target = lax.rem(gx + j, groups)
        copy = pltpu.make_async_remote_copy(
            src_ref=mine.at[:, target],
            dst_ref=got_x.at[gx],
            send_sem=send_sem.at[j], recv_sem=recv_sem.at[j],
            device_id=(model, target, gz), device_id_type=MESH,
        )
        copy.start()
        copies.append(copy)
    def third(z, carry):
        values = inner_velocity(z, middle, eta, density, inverse)
        for f in range(3):
            result[f, z] = values[f]
        return carry

    lax.fori_loop(0, depth, third, 0)
    for row, halo, eta_halo, out, later in edges:
        receive([x_rest2], row)
        values = edge_velocity((0, 1, 2), row, middle, eta, later, eta_halo, density, inverse)
        for f in range(3):
            result[f, :, row] = values[f]
    all_sent([x_u, x_p, x_eta, x_rest, x_u2, x_rest2])

    slot = gz * groups + gx
    index_x = lax.broadcasted_iota(jnp.int32, (16, total_x), 1)
    index_y = lax.broadcasted_iota(jnp.int32, (16, total_x), 0) + 16 * slot
    wx, wy = wave_of(index_x, total_x), wave_of(index_y, NY)
    scale = gravity_scale * layer_depth / (total_x * NY)
    weight = scale * jnp.exp((-0.5 * layer_depth) * jnp.sqrt(wx * wx + wy * wy))
    weight = weight * jnp.where(index_y == 0, jnp.where(index_x == 0, 0.0, 1.0), 2.0)
    weight = jnp.concatenate([weight, weight], axis=1)
    summed = mine[:, gx]
    for j, copy in zip(distant, copies):
        copy.wait_recv()
        summed = summed + got_x[lax.rem(gx + groups - j, groups)]
    high, low = split_value(summed.reshape(16, 2 * total_x) * weight)
    both = dot(jnp.concatenate([high, low], axis=0), bx[0])
    columns = both[:16] + both[16:] + dot(high, bx[1])

    lane = lax.broadcasted_iota(jnp.int32, (8, 128), 1)
    span = 2 * width
    for target in range(groups):
        place = span * target
        group, offset = place // 128 * 128, place % 128
        upper = pltpu.roll(columns[:8, group : group + 128], (128 - offset) % 128, 1)
        lower = pltpu.roll(columns[8:, group : group + 128], (128 + span - offset) % 128, 1)
        back[target] = jnp.where(lane < span, upper, lower)
    returns = []
    for j in sorted(range(1, ranks), key=lambda j: -min(j, ranks - j)):
        other = lax.rem(rank + j, ranks)
        copy = pltpu.make_async_remote_copy(
            src_ref=back.at[other // layers],
            dst_ref=got_back.at[slot],
            send_sem=send_sem2.at[j], recv_sem=recv_sem2.at[j],
            device_id=(model, other // layers, lax.rem(other, layers)), device_id_type=MESH,
        )
        copy.start()
        returns.append(copy)
    got_back[slot] = back[gx]
    for copy in returns:
        copy.wait_recv()
    waves = jnp.transpose(got_back[...].reshape(8 * ranks, 128))
    waves_out[...] = jnp.concatenate(
        [waves[i * width : (i + 1) * width] for i in (0, 2, 1, 3)], axis=1
    )
    for copy in copies + returns:
        copy.wait_send()


def last_kernel(result, waves, ty, velocity_out, pressure_out, gravity, sem):
    outs = [
        pltpu.make_async_copy(result.at[pl.ds(0, 3)], velocity_out, sem.at[0]),
        pltpu.make_async_copy(result.at[3], pressure_out, sem.at[1]),
    ]
    for copy in outs:
        copy.start()
    width = waves.shape[0]
    high, low = split_value(waves[...])
    both = dot_turned(jnp.concatenate([high, low], axis=0), ty[0])
    gravity[...] = both[:width] + both[width:] + dot_turned(high, ty[1])
    for copy in outs:
        copy.wait()


def fused_body(phases, velocity, pressure, density_table, viscosity_table):
    depth, width, lateral = pressure.shape
    groups, layers = lax.axis_size("gx"), lax.axis_size("gz")
    total_x = groups * width
    ty, along_x, phase, bx = host_tables(groups, layers, width, total_x)
    ranks = groups * layers
    f32, b16 = jnp.float32, jnp.bfloat16
    vmem = pl.BlockSpec(memory_space=pltpu.VMEM)
    smem = pl.BlockSpec(memory_space=pltpu.SMEM)
    anywhere = pl.BlockSpec(memory_space=pl.ANY)
    hbm = pl.BlockSpec(memory_space=pltpu.HBM)
    rows = pltpu.VMEM((4, depth, lateral), f32)
    eta_rows = pltpu.VMEM((depth, lateral), f32)
    cells = (depth, width, lateral)
    sems = pltpu.SemaphoreType.DMA
    along_y = jnp.asarray(ty)
    result, waves = pl.pallas_call(
        functools.partial(kernel, groups, layers),
        out_shape=(
            pltpu.VMEM((4,) + cells, f32),
            pltpu.VMEM((width, 2 * HALF_MODES), f32),
        ),
        in_specs=[smem, smem] + [hbm] * 7,
        out_specs=(vmem, vmem),
        scratch_shapes=[
            pltpu.VMEM(cells, jnp.int32),
            pltpu.VMEM((4, depth + 2, width, lateral), f32),
            pltpu.VMEM((depth + 2, width, lateral), f32),
            pltpu.VMEM((4, depth + 2, width, lateral), f32),
            pltpu.VMEM(cells, f32),
            pltpu.VMEM(cells, f32),
            rows, rows, rows, rows, rows, rows, rows, rows,
            eta_rows, eta_rows, eta_rows, eta_rows,
            pltpu.VMEM(ty.shape, b16),
            pltpu.VMEM(along_x.shape, b16),
            pltpu.VMEM(phase.shape, f32),
            pltpu.VMEM(bx.shape, b16),
            pltpu.VMEM(cells, f32),
            pltpu.VMEM((2, ranks, 8, 2 * total_x), f32),
            pltpu.VMEM((2, groups, 8, 2 * total_x), f32),
            pltpu.VMEM((2, groups, 8, 2 * total_x), f32),
            pltpu.VMEM((groups, 2, 8, 2 * total_x), f32),
            pltpu.VMEM((groups, 8, 128), f32),
            pltpu.VMEM((ranks, 8, 128), f32),
            sems((7,)), sems((6,)), sems((24,)), sems((2,)),
            sems((groups,)), sems((groups,)), sems((ranks,)), sems((ranks,)),
        ],
        compiler_params=pltpu.CompilerParams(
            collective_id=0, has_side_effects=True, vmem_limit_bytes=56 * 1024 * 1024
        ),
    )(
        density_table, viscosity_table, phases, velocity, pressure,
        along_y, jnp.asarray(along_x), jnp.asarray(phase), jnp.asarray(bx),
    )
    return pl.pallas_call(
        last_kernel,
        out_shape=(
            jax.ShapeDtypeStruct(velocity.shape, f32),
            jax.ShapeDtypeStruct(pressure.shape, f32),
            jax.ShapeDtypeStruct((width, lateral), f32),
        ),
        in_specs=[vmem] * 3,
        out_specs=(hbm, hbm, vmem),
        scratch_shapes=[sems((2,))],
        compiler_params=pltpu.CompilerParams(vmem_limit_bytes=16 * 1024 * 1024),
    )(result, waves, along_y)


def local_program(phases, velocity, pressure, density_table, viscosity_table):
    depth, width, lateral = pressure.shape
    groups, layers = lax.axis_size("gx"), lax.axis_size("gz")
    fits = layers == 2 and groups * width == 128 and width == 16 and depth % 8 == 0
    chosen = fused_body if fits else body
    return chosen(phases, velocity, pressure, density_table, viscosity_table)


def solution(mesh):
    in_specs = (
        P(("models", "gz"), "gx", None),
        P(None, ("models", "gz"), "gx", None),
        P(("models", "gz"), "gx", None),
        P(),
        P(),
    )
    out_specs = (
        P(None, ("models", "gz"), "gx", None),
        P(("models", "gz"), "gx", None),
        P(("models", "gx"), None),
    )
    return jax.shard_map(local_program, mesh=mesh, in_specs=in_specs, out_specs=out_specs, check_vma=False)
```

```python
import functools
import math

import jax
import jax.numpy as jnp
import numpy as np
from jax import lax
from jax.experimental import pallas as pl
from jax.experimental.pallas import tpu as pltpu
from jax.sharding import PartitionSpec as P

NY = 512
ITERS = 2


velocity_rate = 0.1
pressure_rate = 0.5
bulk_time = 2.0
shear_time = 4.0
squeeze = 0.25
gravity_scale = 4.0
layer_depth = 0.125
highest = lax.Precision.HIGHEST


def with_halo(block, sides, width):
    for axis, dim in sides:
        count = lax.axis_size(axis)
        forward = [(i, i + 1) for i in range(count - 1)]
        backward = [(target, source) for source, target in forward]
        low = lax.ppermute(
            lax.slice_in_dim(block, block.shape[dim] - width, None, axis=dim), axis, forward
        )
        high = lax.ppermute(lax.slice_in_dim(block, 0, width, axis=dim), axis, backward)
        block = jnp.concatenate([low, block, high], axis=dim)
    return block


def neighbour(field, dim_index, offset):
    lead_count = field.ndim - 3
    pieces = [slice(None)] * lead_count + [slice(1, -1), slice(1, -1), slice(1, -1)]
    pieces[lead_count + dim_index] = slice(2, None) if offset > 0 else slice(0, -2)
    return field[tuple(pieces)]


def center(field):
    lead_count = field.ndim - 3
    pieces = [slice(None)] * lead_count + [slice(1, -1), slice(1, -1), slice(1, -1)]
    return field[tuple(pieces)]


def relaxation(fields, viscous, density, previous):
    padded = jnp.pad(fields, ((0, 0), (0, 0), (0, 0), (1, 1)))
    eta_full = jnp.pad(viscous, ((0, 0), (0, 0), (1, 1)))
    eta_core = center(eta_full)
    pressure_full = padded[3]
    results = []
    for component, dim_index in ((0, 1), (1, 2), (2, 0)):
        moving = padded[component]
        moving_core = center(moving)
        stress = jnp.zeros_like(moving_core)
        for facing in range(3):
            for offset in (1, -1):
                face_eta = 0.5 * (eta_core + neighbour(eta_full, facing, offset))
                stress = stress + face_eta * (neighbour(moving, facing, offset) - moving_core)
        forcing = stress - 0.5 * (
            neighbour(pressure_full, dim_index, 1) - neighbour(pressure_full, dim_index, -1)
        )
        if component == 2:
            forcing = forcing - density[1:-1, 1:-1, :]
        results.append(moving_core + velocity_rate * forcing / eta_core)
    spread = jnp.zeros_like(eta_core)
    for component, dim_index in ((0, 1), (1, 2), (2, 0)):
        spread = spread + 0.5 * (
            neighbour(padded[component], dim_index, 1) - neighbour(padded[component], dim_index, -1)
        )
    pressure_core = center(pressure_full)
    results.append(
        pressure_core
        - pressure_rate * (spread + (pressure_core - previous[1:-1, 1:-1, :]) / bulk_time)
    )
    return jnp.stack(results)


def dft_table(row_count, col_count, period):
    row_index = jnp.arange(row_count, dtype=jnp.int32)[:, None]
    col_index = jnp.arange(col_count, dtype=jnp.int32)[None, :]
    angles = (row_index * col_index % period).astype(jnp.float32) * (2.0 * math.pi / period)
    return (jnp.cos(angles), jnp.sin(angles))


def combine(plain_part, turned, orientation):
    real_part = plain_part[:, :, 0] - orientation * turned[:, :, 1]
    imag_part = plain_part[:, :, 1] + orientation * turned[:, :, 0]
    return jnp.stack([real_part, imag_part], axis=2)


def transform(columns, orientation):
    length = columns.shape[0]
    width_cols = columns.shape[2]
    inner_size = math.gcd(length, 128)
    outer_size = length // inner_size
    blocks = columns.reshape(inner_size, outer_size, 2, width_cols)
    cosine_table, sine_table = dft_table(inner_size, inner_size, inner_size)
    plain_part = jnp.einsum("bajm,bk->kajm", blocks, cosine_table, precision=highest)
    turned = jnp.einsum("bajm,bk->kajm", blocks, sine_table, precision=highest)
    blocks = combine(plain_part, turned, orientation)
    twist_cos, twist_sin = dft_table(inner_size, outer_size, length)
    twist_cos = twist_cos[:, :, None]
    twist_sin = twist_sin[:, :, None]
    real_part = blocks[:, :, 0]
    imag_part = blocks[:, :, 1]
    blocks = jnp.stack(
        [
            real_part * twist_cos - orientation * imag_part * twist_sin,
            imag_part * twist_cos + orientation * real_part * twist_sin,
        ],
        axis=2,
    )
    cosine_table, sine_table = dft_table(outer_size, outer_size, outer_size)
    plain_part = jnp.einsum("kajm,al->lkjm", blocks, cosine_table, precision=highest)
    turned = jnp.einsum("kajm,al->lkjm", blocks, sine_table, precision=highest)
    return combine(plain_part, turned, orientation).reshape(length, 2, width_cols)


def centered_wave(index_of, length):
    shifted = jnp.where(index_of < length // 2, index_of, index_of - length)
    return shifted.astype(jnp.float32) * (2.0 * math.pi / length)


def forward_rows(loaded, mode_count, groups):
    lateral = loaded.shape[2]
    local_modes = mode_count // groups
    cosine_table, sine_table = dft_table(lateral, mode_count, lateral)
    cos_blocks = cosine_table.reshape(lateral, groups, local_modes)
    sin_blocks = sine_table.reshape(lateral, groups, local_modes)
    real_part = jnp.einsum("zxy,ygk->gxzk", loaded, cos_blocks, precision=highest)
    imag_part = -jnp.einsum("zxy,ygk->gxzk", loaded, sin_blocks, precision=highest)
    return jnp.stack([real_part, imag_part], axis=2).reshape(groups, -1)


def fold_depth(received, mode_count, groups, width_cells, depth_cells):
    local_modes = mode_count // groups
    total_x = groups * width_cells
    columns = received.reshape(total_x, 2, depth_cells * local_modes)
    spectrum = transform(columns, -1.0).reshape(total_x, 2, depth_cells, local_modes)
    index_x = jnp.arange(total_x, dtype=jnp.int32)
    index_y = lax.axis_index("gx") * local_modes + jnp.arange(local_modes, dtype=jnp.int32)
    wave_x = centered_wave(index_x, total_x)
    wave_y = centered_wave(index_y, NY)
    magnitude = jnp.sqrt(wave_x[:, None] ** 2 + wave_y[None, :] ** 2)
    depth_of = (
        lax.axis_index("gz") * depth_cells + jnp.arange(depth_cells, dtype=jnp.int32)
    ).astype(jnp.float32)
    depth_of = (depth_of + 0.5) * layer_depth
    retained = (
        (index_y != NY // 2)[None, :]
        & jnp.logical_not((index_x == 0)[:, None] & (index_y == 0)[None, :])
    ).astype(jnp.float32)
    weights = (
        gravity_scale
        * layer_depth
        * jnp.exp(-magnitude[:, None, :] * depth_of[None, :, None])
        * retained[:, None, :]
    )
    partial_value = jnp.sum(weights[:, None] * spectrum, axis=2)
    summed = lax.psum(partial_value, "gz")
    restored = transform(summed, 1.0)
    return restored.reshape(groups, width_cells * 2 * local_modes)


def finish(returned, mode_count, groups, width_cells):
    local_modes = mode_count // groups
    columns = returned.reshape(groups, width_cells, 2, local_modes)
    mode_index = jnp.arange(mode_count, dtype=jnp.int32)
    factor = jnp.where(mode_index == 0, 1.0, 1.0)
    cosine_table, sine_table = dft_table(mode_count, NY, NY)
    cos_blocks = (factor[:, None] * cosine_table).reshape(groups, local_modes, NY)
    sin_blocks = (factor[:, None] * sine_table).reshape(groups, local_modes, NY)
    real_sum = jnp.einsum("sxk,sky->xy", columns[:, :, 0], cos_blocks, precision=highest)
    imag_sum = jnp.einsum("sxk,sky->xy", columns[:, :, 1], sin_blocks, precision=highest)
    return (real_sum - imag_sum) / (groups * width_cells * NY)


def body(phases, velocity, pressure, density_table, viscosity_table):
    classes = jnp.arange(density_table.shape[0], dtype=jnp.int32)[:, None, None, None]
    chosen = phases[None] == classes
    density = jnp.sum(jnp.where(chosen, density_table[:, None, None, None], 0.0), axis=0)
    viscosity = jnp.sum(jnp.where(chosen, viscosity_table[:, None, None, None], 0.0), axis=0)
    effective = 1.0 / (1.0 / viscosity + 1.0 / shear_time)
    depth_cells, width_cells, lateral = pressure.shape
    groups = lax.axis_size("gx")
    fields = jnp.concatenate([velocity, pressure[None]], axis=0)
    margin = ((1, 1), (1, 1), (0, 0))
    for sweeps in range(ITERS):
        stacked = jnp.concatenate([fields, effective[None]], axis=0)
        widened = with_halo(stacked, (("gx", 2), ("gz", 1)), 1)
        fields = relaxation(
            widened[:4], widened[4], jnp.pad(density, margin), jnp.pad(pressure, margin)
        )
    velocity_out = fields[:3]
    pressure_out = fields[3]
    loaded = density * (1.0 + squeeze * pressure_out)
    packed = forward_rows(loaded, lateral, groups)
    received = lax.all_to_all(packed, "gx", split_axis=0, concat_axis=0, tiled=True)
    folded = fold_depth(received, lateral, groups, width_cells, depth_cells)
    returned = lax.all_to_all(folded, "gx", split_axis=0, concat_axis=0, tiled=True)
    gravity = finish(returned, lateral, groups, width_cells)
    return (velocity_out, pressure_out, gravity)


HALF_MODES = NY // 2
MESH = pl.DeviceIdType.MESH


def split_table(table):
    high = table.astype(jnp.bfloat16)
    low = (table - high.astype(np.float32)).astype(jnp.bfloat16)
    return high, low


def host_tables(layers, width, total_x):
    y = np.arange(NY)[:, None]
    k = np.arange(HALF_MODES)[None, :]
    angle = (y * k % NY) * (2.0 * np.pi / NY)
    along_y = np.stack(
        [part.reshape(NY, layers, -1) for part in (np.cos(angle), -np.sin(angle))], axis=2
    ).reshape(NY, 2 * HALF_MODES).astype(np.float32)
    kx = np.arange(total_x)[:, None]
    local = np.arange(width)[None, :]
    angle = (kx * local % total_x) * (2.0 * np.pi / total_x)
    c, s = np.cos(angle), np.sin(angle)
    along_x = np.block([[c, s], [-s, c]]).astype(np.float32)
    high, low = split_table(along_x)
    along_x = np.concatenate([high, high, low], axis=1)
    x = np.arange(total_x)[None, :]
    angle = (kx * x % total_x) * (2.0 * np.pi / total_x)
    c, s = np.cos(angle), np.sin(angle)
    back_x = np.block([[c, -s], [s, c]]).astype(np.float32)
    return np.stack(split_table(along_y)), along_x, np.stack(split_table(back_x))


def split_value(value):
    high = value.astype(jnp.bfloat16)
    low = (value - high.astype(jnp.float32)).astype(jnp.bfloat16)
    return high, low


def dot(left, right):
    return jnp.dot(left, right, preferred_element_type=jnp.float32)


def dot_turned(left, right):
    return lax.dot_general(
        left, right, (((1,), (1,)), ((), ())), preferred_element_type=jnp.float32
    )


def wave_of(index, length):
    shifted = jnp.where(index < length // 2, index, index - length)
    return shifted.astype(jnp.float32) * (2.0 * math.pi / length)


def new_velocity(f, value, side, faces, gradient, density, inverse):
    flux = faces[0] * side[0]
    for n in range(1, 6):
        flux = flux + faces[n] * side[n]
    forcing = flux - sum(faces[1:], faces[0]) * value - gradient
    if f == 2:
        forcing = forcing - 2.0 * density
    return value + (0.5 * velocity_rate) * inverse * forcing


def new_pressure(value, spread, start):
    return value - pressure_rate * (0.5 * spread + (value - start) / bulk_time)


def beside_y(tile):
    lateral = tile.shape[1]
    lane = lax.broadcasted_iota(jnp.int32, tile.shape, 1)
    return (
        jnp.where(lane == lateral - 1, 0.0, pltpu.roll(tile, lateral - 1, 1)),
        jnp.where(lane == 0, 0.0, pltpu.roll(tile, 1, 1)),
    )


def beside_plane(ref, lead, z):
    plane = ref[lead + (z + 1,)]
    width = plane.shape[0]
    ahead, behind = beside_y(plane)
    return plane, (
        pltpu.roll(plane, width - 1, 0), pltpu.roll(plane, 1, 0), ahead, behind,
        ref[lead + (z + 2,)], ref[lead + (z,)],
    )


def inner_velocity(z, block, eta, density, inverse):
    center, others = beside_plane(eta, (), z)
    faces = [center + other for other in others]
    pairs = [beside_plane(block, (f,), z) for f in range(4)]
    push = pairs[3][1]
    return [
        new_velocity(
            f, pairs[f][0], pairs[f][1], faces, push[2 * f] - push[2 * f + 1], density[z], inverse[z]
        )
        for f in range(3)
    ]


def inner_pressure(z, block, start):
    width = block.shape[2]
    along_x, along_y = block[0, z + 1], block[1, z + 1]
    ahead, behind = beside_y(along_y)
    spread = pltpu.roll(along_x, width - 1, 0) - pltpu.roll(along_x, 1, 0)
    spread = spread + (ahead - behind) + (block[2, z + 2] - block[2, z])
    return new_pressure(block[3, z + 1], spread, start[3, z + 1])


def beside_row(ref, lead, row, outer):
    depth = ref.shape[-3] - 2
    tile = ref[lead + (slice(1, depth + 1), row)]
    layer = lax.broadcasted_iota(jnp.int32, tile.shape, 0)
    below = jnp.where(layer == 0, ref[lead + (slice(0, 1), row)], pltpu.roll(tile, 1, 0))
    above = jnp.where(
        layer == depth - 1,
        ref[lead + (slice(depth + 1, depth + 2), row)],
        pltpu.roll(tile, depth - 1, 0),
    )
    ahead, behind = beside_y(tile)
    inner = ref[lead + (slice(1, depth + 1), row + 1 if row == 0 else row - 1)]
    along = (inner, outer) if row == 0 else (outer, inner)
    return tile, along + (ahead, behind, above, below)


def edge_velocity(wanted, row, block, eta, halo, eta_halo, density, inverse):
    center, others = beside_row(eta, (), row, eta_halo[...])
    faces = [center + other for other in others]
    push = beside_row(block, (3,), row, halo[3])[1]
    results = []
    for f in wanted:
        value, side = beside_row(block, (f,), row, halo[f])
        results.append(
            new_velocity(
                f, value, side, faces, push[2 * f] - push[2 * f + 1], density[:, row],
                inverse[:, row],
            )
        )
    return results


def edge_pressure(row, block, halo, start):
    depth = block.shape[1] - 2
    spread = None
    for f in range(3):
        side = beside_row(block, (f,), row, halo[f])[1]
        change = side[2 * f] - side[2 * f + 1]
        spread = change if spread is None else spread + change
    here = slice(1, depth + 1)
    return new_pressure(block[3, here, row], spread, start[3, here, row])


def kernel(
    groups, layers,
    dens_ref, visc_ref, phases_hbm, velocity_hbm, pressure_hbm,
    ty_hbm, along_x_hbm, bx_hbm,
    result, waves_out,
    ph, fields, eta, middle, density, inverse,
    send_low, send_high, get_low, get_high, send_low2, send_high2, get_low2, get_high2,
    eta_send_low, eta_send_high, eta_low, eta_high,
    ty, along_x, bx,
    loaded, partial, got_z, mine, got_x, whole,
    load_sem, z_sem, x_sem, pair_sem, send_sem, recv_sem,
):
    model, gx, gz = lax.axis_index("models"), lax.axis_index("gx"), lax.axis_index("gz")
    depth, width, lateral = density.shape
    total_x = groups * width
    ranks = groups * layers
    rank = gx * layers + gz
    last = width - 1

    loads = [
        pltpu.make_async_copy(src, dst, load_sem.at[i])
        for i, (src, dst) in enumerate(
            [
                (velocity_hbm, fields.at[pl.ds(0, 3), pl.ds(1, depth)]),
                (pressure_hbm, fields.at[3, pl.ds(1, depth)]),
                (phases_hbm, ph),
                (ty_hbm, ty),
                (along_x_hbm, along_x),
                (bx_hbm, bx),
            ]
        )
    ]
    for copy in loads[:3]:
        copy.start()

    barrier = pltpu.get_barrier_semaphore()
    for j in range(1, ranks):
        other = lax.rem(rank + j, ranks)
        pl.semaphore_signal(
            barrier, inc=1, device_id=(model, other // layers, lax.rem(other, layers)),
            device_id_type=MESH,
        )

    edge = (depth + 1) * gz
    empty = jnp.zeros((width, lateral), jnp.float32)
    eta[edge] = empty
    for f in range(4):
        fields[f, edge] = empty
        middle[f, edge] = empty

    @pl.when(gx == 0)
    def _():
        for ref in (get_low, get_low2, eta_low):
            ref[...] = jnp.zeros_like(ref)

    @pl.when(gx == groups - 1)
    def _():
        for ref in (get_high, get_high2, eta_high):
            ref[...] = jnp.zeros_like(ref)

    def beside_x(stage, out_low, out_high, in_low, in_high):
        down = pltpu.make_async_remote_copy(
            src_ref=out_low, dst_ref=in_high,
            send_sem=x_sem.at[4 * stage], recv_sem=x_sem.at[4 * stage + 1],
            device_id=(model, lax.rem(gx + groups - 1, groups), gz), device_id_type=MESH,
        )
        up = pltpu.make_async_remote_copy(
            src_ref=out_high, dst_ref=in_low,
            send_sem=x_sem.at[4 * stage + 2], recv_sem=x_sem.at[4 * stage + 3],
            device_id=(model, lax.rem(gx + 1, groups), gz), device_id_type=MESH,
        )
        return down, up

    def send(pairs, rows=(0, last)):
        if 0 in rows:
            @pl.when(gx > 0)
            def _():
                for down, up in pairs:
                    down.start()

        if last in rows:
            @pl.when(gx < groups - 1)
            def _():
                for down, up in pairs:
                    up.start()

    def receive(pairs, row):
        if row == 0:
            @pl.when(gx > 0)
            def _():
                for down, up in pairs:
                    up.wait_recv()
        else:
            @pl.when(gx < groups - 1)
            def _():
                for down, up in pairs:
                    down.wait_recv()

    def all_sent(pairs):
        @pl.when(gx > 0)
        def _():
            for down, up in pairs:
                down.wait_send()

        @pl.when(gx < groups - 1)
        def _():
            for down, up in pairs:
                up.wait_send()

    def beside_z(stage, source, target):
        copy = pltpu.make_async_remote_copy(
            src_ref=source, dst_ref=target,
            send_sem=z_sem.at[2 * stage], recv_sem=z_sem.at[2 * stage + 1],
            device_id=(model, gx, 1 - gz), device_id_type=MESH,
        )
        copy.start()
        return copy

    bundle = (send_low, send_high, get_low, get_high)
    bundle2 = (send_low2, send_high2, get_low2, get_high2)
    x_u = beside_x(0, *[ref.at[0] for ref in bundle])
    x_p = beside_x(1, *[ref.at[3] for ref in bundle])
    x_eta = beside_x(2, eta_send_low, eta_send_high, eta_low, eta_high)
    x_rest = beside_x(3, *[ref.at[pl.ds(1, 2)] for ref in bundle])
    x_u2 = beside_x(4, *[ref.at[0] for ref in bundle2])
    x_rest2 = beside_x(5, *[ref.at[pl.ds(1, 3)] for ref in bundle2])
    edges = (
        (0, get_low, eta_low, send_low2, get_low2),
        (last, get_high, eta_high, send_high2, get_high2),
    )

    facing = depth - (depth - 1) * gz
    loads[0].wait()
    loads[1].wait()
    for f in range(4):
        send_low[f] = fields[f, 1 : depth + 1, 0]
        send_high[f] = fields[f, 1 : depth + 1, last]
    pl.semaphore_wait(barrier, ranks - 1)
    send([x_u, x_p])
    z_first = beside_z(0, fields.at[:, facing], fields.at[:, edge])

    loads[2].wait()
    for copy in loads[3:]:
        copy.start()

    def look_up(z, carry):
        kind = ph[z]
        dens = jnp.full(kind.shape, dens_ref[0], jnp.float32)
        visc = jnp.full(kind.shape, visc_ref[0], jnp.float32)
        for c in range(1, dens_ref.shape[0]):
            here = kind == c
            dens = jnp.where(here, dens_ref[c], dens)
            visc = jnp.where(here, visc_ref[c], visc)
        inv = 1.0 / visc + 1.0 / shear_time
        density[z] = dens
        inverse[z] = inv
        eta[z + 1] = 1.0 / inv
        return carry

    lax.fori_loop(0, depth, look_up, 0)
    eta_send_low[...] = eta[1 : depth + 1, 0]
    eta_send_high[...] = eta[1 : depth + 1, last]
    send([x_eta, x_rest])
    z_eta = beside_z(1, eta.at[facing], eta.at[edge])
    z_first.wait()
    z_eta.wait()

    def first(z, carry):
        values = inner_velocity(z, fields, eta, density, inverse)
        for f in range(3):
            middle[f, z + 1] = values[f]
        middle[3, z + 1] = inner_pressure(z, fields, fields)
        return carry

    lax.fori_loop(0, depth, first, 0)

    for row, halo, eta_halo, out, later in edges:
        receive([x_u, x_p, x_eta], row)
        out[0] = edge_velocity((0,), row, fields, eta, halo, eta_halo, density, inverse)[0]
        send([x_u2], (row,))
    for row, halo, eta_halo, out, later in edges:
        receive([x_rest], row)
        out[1], out[2] = edge_velocity(
            (1, 2), row, fields, eta, halo, eta_halo, density, inverse
        )
        out[3] = edge_pressure(row, fields, halo, fields)
    for row, halo, eta_halo, out, later in edges:
        for f in range(4):
            middle[f, 1 : depth + 1, row] = out[f]
    z_second = beside_z(2, middle.at[:, facing], middle.at[:, edge])
    send([x_rest2])
    z_second.wait()

    def second(z, carry):
        pressure = inner_pressure(z, middle, fields)
        result[3, z] = pressure
        loaded[z] = density[z] * (1.0 + squeeze * pressure)
        return carry

    lax.fori_loop(0, depth, second, 0)

    index_x = lax.broadcasted_iota(jnp.int32, (total_x, HALF_MODES), 0)
    index_y = lax.broadcasted_iota(jnp.int32, (total_x, HALF_MODES), 1)
    wx, wy = wave_of(index_x, total_x), wave_of(index_y, NY)
    magnitude = jnp.sqrt(wx * wx + wy * wy)
    decay = jnp.exp(-layer_depth * magnitude)
    top = layer_depth * (0.5 + depth * gz.astype(jnp.float32))
    scale = gravity_scale * layer_depth / (total_x * NY)
    weight = scale * jnp.exp(-top * magnitude)
    weight = weight * jnp.where(index_y == 0, jnp.where(index_x == 0, 0.0, 1.0), 2.0)
    for copy in loads[3:]:
        copy.wait()
    for row, halo, eta_halo, out, later in edges:
        receive([x_u2], row)
        pressure = edge_pressure(row, middle, later, fields)
        result[3, :, row] = pressure
        loaded[:, row] = density[:, row] * (1.0 + squeeze * pressure)

    high, low = split_value(loaded[...].reshape(depth * width, lateral))
    both = dot(jnp.concatenate([high, low], axis=0), ty[0])
    rows = both[: depth * width] + both[depth * width :] + dot(high, ty[1])
    held = HALF_MODES // layers
    parts = [rows[:, held * i : held * (i + 1)] for i in range(2 * layers)]
    real = jnp.concatenate(parts[0::2], axis=1)
    imag = jnp.concatenate(parts[1::2], axis=1)
    decay = jnp.concatenate([decay, decay], axis=0)
    weights = along_x[...]
    total = None
    for z in range(depth - 1, -1, -1):
        here = slice(z * width, (z + 1) * width)
        layer = jnp.concatenate([real[here], imag[here]], axis=0)
        high, low = split_value(layer)
        spectrum = dot(weights, jnp.concatenate([high, low, high], axis=0))
        total = spectrum if total is None else total * decay + spectrum

    high, low = split_value(total * jnp.concatenate([weight, weight], axis=0))
    both = dot(bx[0], jnp.concatenate([high, low], axis=1))
    field = both[:, :HALF_MODES] + both[:, HALF_MODES:] + dot(bx[1], high)
    for i in range(layers):
        partial[i] = field[:, held * i : held * (i + 1)].reshape(2, groups, width, held)

    near = groups // 4
    spans = [(near, groups - 2 * near), (0, near), (groups - near, near)]
    across = []
    for i, (begin, count) in enumerate(spans):
        block = pl.ds(begin, count)
        copy = pltpu.make_async_remote_copy(
            src_ref=partial.at[1 - gz, :, block],
            dst_ref=got_z.at[:, block],
            send_sem=pair_sem.at[2 * i], recv_sem=pair_sem.at[2 * i + 1],
            device_id=(model, gx, 1 - gz), device_id_type=MESH,
        )
        copy.start()
        across.append(copy)
    copies = []
    for (begin, count), arrival in zip(spans, across):
        block = pl.ds(begin, count)
        arrival.wait_recv()
        mine[:, block] = partial[gz, :, block] + got_z[:, block]
        offsets = range(max(begin, 1), begin + count)
        for j in sorted(offsets, key=lambda j: -min(j, groups - j)):
            copy = pltpu.make_async_remote_copy(
                src_ref=mine.at[:, j],
                dst_ref=got_x.at[j],
                send_sem=send_sem.at[j], recv_sem=recv_sem.at[j],
                device_id=(model, lax.rem(gx + j, groups), gz), device_id_type=MESH,
            )
            copy.start()
            copies.append((j, copy))

    def third(z, carry):
        values = inner_velocity(z, middle, eta, density, inverse)
        for f in range(3):
            result[f, z] = values[f]
        return carry

    lax.fori_loop(0, depth, third, 0)
    for row, halo, eta_halo, out, later in edges:
        receive([x_rest2], row)
        values = edge_velocity((0, 1, 2), row, middle, eta, later, eta_halo, density, inverse)
        for f in range(3):
            result[f, :, row] = values[f]
    all_sent([x_u, x_p, x_eta, x_rest, x_u2, x_rest2])

    summed = mine[:, 0]
    for j, copy in copies:
        copy.wait_recv()
        summed = summed + got_x[j]
    whole[gz] = summed
    last_copy = pltpu.make_async_remote_copy(
        src_ref=whole.at[gz], dst_ref=whole.at[gz],
        send_sem=pair_sem.at[6], recv_sem=pair_sem.at[7],
        device_id=(model, gx, 1 - gz), device_id_type=MESH,
    )
    last_copy.start()
    for j, copy in copies:
        copy.wait_send()
    for copy in across:
        copy.wait_send()
    last_copy.wait()
    waves_out[...] = jnp.concatenate(
        [whole[i, part] for i in range(layers) for part in range(2)], axis=1
    )


def last_kernel(result, waves, ty, velocity_out, pressure_out, gravity, sem):
    outs = [
        pltpu.make_async_copy(result.at[pl.ds(0, 3)], velocity_out, sem.at[0]),
        pltpu.make_async_copy(result.at[3], pressure_out, sem.at[1]),
    ]
    for copy in outs:
        copy.start()
    width = waves.shape[0]
    high, low = split_value(waves[...])
    both = dot_turned(jnp.concatenate([high, low], axis=0), ty[0])
    gravity[...] = both[:width] + both[width:] + dot_turned(high, ty[1])
    for copy in outs:
        copy.wait()


def fused_body(phases, velocity, pressure, density_table, viscosity_table):
    depth, width, lateral = pressure.shape
    groups, layers = lax.axis_size("gx"), lax.axis_size("gz")
    total_x = groups * width
    ty, along_x, bx = host_tables(layers, width, total_x)
    held = HALF_MODES // layers
    shares = pltpu.VMEM((2, groups, width, held), jnp.float32)
    f32, b16 = jnp.float32, jnp.bfloat16
    vmem = pl.BlockSpec(memory_space=pltpu.VMEM)
    smem = pl.BlockSpec(memory_space=pltpu.SMEM)
    anywhere = pl.BlockSpec(memory_space=pl.ANY)
    hbm = pl.BlockSpec(memory_space=pltpu.HBM)
    rows = pltpu.VMEM((4, depth, lateral), f32)
    eta_rows = pltpu.VMEM((depth, lateral), f32)
    cells = (depth, width, lateral)
    sems = pltpu.SemaphoreType.DMA
    along_y = jnp.asarray(ty)
    result, waves = pl.pallas_call(
        functools.partial(kernel, groups, layers),
        out_shape=(
            pltpu.VMEM((4,) + cells, f32),
            pltpu.VMEM((width, 2 * HALF_MODES), f32),
        ),
        in_specs=[smem, smem] + [hbm] * 6,
        out_specs=(vmem, vmem),
        scratch_shapes=[
            pltpu.VMEM(cells, jnp.int32),
            pltpu.VMEM((4, depth + 2, width, lateral), f32),
            pltpu.VMEM((depth + 2, width, lateral), f32),
            pltpu.VMEM((4, depth + 2, width, lateral), f32),
            pltpu.VMEM(cells, f32),
            pltpu.VMEM(cells, f32),
            rows, rows, rows, rows, rows, rows, rows, rows,
            eta_rows, eta_rows, eta_rows, eta_rows,
            pltpu.VMEM(ty.shape, b16),
            pltpu.VMEM(along_x.shape, b16),
            pltpu.VMEM(bx.shape, b16),
            pltpu.VMEM(cells, f32),
            pltpu.VMEM((layers, 2, groups, width, held), f32),
            shares, shares,
            pltpu.VMEM((groups, 2, width, held), f32),
            pltpu.VMEM((layers, 2, width, held), f32),
            sems((6,)), sems((6,)), sems((24,)), sems((8,)),
            sems((groups,)), sems((groups,)),
        ],
        compiler_params=pltpu.CompilerParams(
            collective_id=0, has_side_effects=True, vmem_limit_bytes=56 * 1024 * 1024
        ),
    )(
        density_table, viscosity_table, phases, velocity, pressure,
        along_y, jnp.asarray(along_x), jnp.asarray(bx),
    )
    return pl.pallas_call(
        last_kernel,
        out_shape=(
            jax.ShapeDtypeStruct(velocity.shape, f32),
            jax.ShapeDtypeStruct(pressure.shape, f32),
            jax.ShapeDtypeStruct((width, lateral), f32),
        ),
        in_specs=[vmem] * 3,
        out_specs=(hbm, hbm, vmem),
        scratch_shapes=[sems((2,))],
        compiler_params=pltpu.CompilerParams(vmem_limit_bytes=16 * 1024 * 1024),
    )(result, waves, along_y)


def local_program(phases, velocity, pressure, density_table, viscosity_table):
    depth, width, lateral = pressure.shape
    groups, layers = lax.axis_size("gx"), lax.axis_size("gz")
    fits = layers == 2 and groups * width == 128 and width == 16 and depth % 8 == 0
    chosen = fused_body if fits else body
    return chosen(phases, velocity, pressure, density_table, viscosity_table)


def solution(mesh):
    in_specs = (
        P(("models", "gz"), "gx", None),
        P(None, ("models", "gz"), "gx", None),
        P(("models", "gz"), "gx", None),
        P(),
        P(),
    )
    out_specs = (
        P(None, ("models", "gz"), "gx", None),
        P(("models", "gz"), "gx", None),
        P(("models", "gx"), None),
    )
    return jax.shard_map(local_program, mesh=mesh, in_specs=in_specs, out_specs=out_specs, check_vma=False)
```

```python
import functools
import math

import jax
import jax.numpy as jnp
import numpy as np
from jax import lax
from jax.experimental import pallas as pl
from jax.experimental.pallas import tpu as pltpu
from jax.sharding import PartitionSpec as P

NY = 512
ITERS = 2


velocity_rate = 0.1
pressure_rate = 0.5
bulk_time = 2.0
shear_time = 4.0
squeeze = 0.25
gravity_scale = 4.0
layer_depth = 0.125
highest = lax.Precision.HIGHEST


def with_halo(block, sides, width):
    for axis, dim in sides:
        count = lax.axis_size(axis)
        forward = [(i, i + 1) for i in range(count - 1)]
        backward = [(target, source) for source, target in forward]
        low = lax.ppermute(
            lax.slice_in_dim(block, block.shape[dim] - width, None, axis=dim), axis, forward
        )
        high = lax.ppermute(lax.slice_in_dim(block, 0, width, axis=dim), axis, backward)
        block = jnp.concatenate([low, block, high], axis=dim)
    return block


def neighbour(field, dim_index, offset):
    lead_count = field.ndim - 3
    pieces = [slice(None)] * lead_count + [slice(1, -1), slice(1, -1), slice(1, -1)]
    pieces[lead_count + dim_index] = slice(2, None) if offset > 0 else slice(0, -2)
    return field[tuple(pieces)]


def center(field):
    lead_count = field.ndim - 3
    pieces = [slice(None)] * lead_count + [slice(1, -1), slice(1, -1), slice(1, -1)]
    return field[tuple(pieces)]


def relaxation(fields, viscous, density, previous):
    padded = jnp.pad(fields, ((0, 0), (0, 0), (0, 0), (1, 1)))
    eta_full = jnp.pad(viscous, ((0, 0), (0, 0), (1, 1)))
    eta_core = center(eta_full)
    pressure_full = padded[3]
    results = []
    for component, dim_index in ((0, 1), (1, 2), (2, 0)):
        moving = padded[component]
        moving_core = center(moving)
        stress = jnp.zeros_like(moving_core)
        for facing in range(3):
            for offset in (1, -1):
                face_eta = 0.5 * (eta_core + neighbour(eta_full, facing, offset))
                stress = stress + face_eta * (neighbour(moving, facing, offset) - moving_core)
        forcing = stress - 0.5 * (
            neighbour(pressure_full, dim_index, 1) - neighbour(pressure_full, dim_index, -1)
        )
        if component == 2:
            forcing = forcing - density[1:-1, 1:-1, :]
        results.append(moving_core + velocity_rate * forcing / eta_core)
    spread = jnp.zeros_like(eta_core)
    for component, dim_index in ((0, 1), (1, 2), (2, 0)):
        spread = spread + 0.5 * (
            neighbour(padded[component], dim_index, 1) - neighbour(padded[component], dim_index, -1)
        )
    pressure_core = center(pressure_full)
    results.append(
        pressure_core
        - pressure_rate * (spread + (pressure_core - previous[1:-1, 1:-1, :]) / bulk_time)
    )
    return jnp.stack(results)


def dft_table(row_count, col_count, period):
    row_index = jnp.arange(row_count, dtype=jnp.int32)[:, None]
    col_index = jnp.arange(col_count, dtype=jnp.int32)[None, :]
    angles = (row_index * col_index % period).astype(jnp.float32) * (2.0 * math.pi / period)
    return (jnp.cos(angles), jnp.sin(angles))


def combine(plain_part, turned, orientation):
    real_part = plain_part[:, :, 0] - orientation * turned[:, :, 1]
    imag_part = plain_part[:, :, 1] + orientation * turned[:, :, 0]
    return jnp.stack([real_part, imag_part], axis=2)


def transform(columns, orientation):
    length = columns.shape[0]
    width_cols = columns.shape[2]
    inner_size = math.gcd(length, 128)
    outer_size = length // inner_size
    blocks = columns.reshape(inner_size, outer_size, 2, width_cols)
    cosine_table, sine_table = dft_table(inner_size, inner_size, inner_size)
    plain_part = jnp.einsum("bajm,bk->kajm", blocks, cosine_table, precision=highest)
    turned = jnp.einsum("bajm,bk->kajm", blocks, sine_table, precision=highest)
    blocks = combine(plain_part, turned, orientation)
    twist_cos, twist_sin = dft_table(inner_size, outer_size, length)
    twist_cos = twist_cos[:, :, None]
    twist_sin = twist_sin[:, :, None]
    real_part = blocks[:, :, 0]
    imag_part = blocks[:, :, 1]
    blocks = jnp.stack(
        [
            real_part * twist_cos - orientation * imag_part * twist_sin,
            imag_part * twist_cos + orientation * real_part * twist_sin,
        ],
        axis=2,
    )
    cosine_table, sine_table = dft_table(outer_size, outer_size, outer_size)
    plain_part = jnp.einsum("kajm,al->lkjm", blocks, cosine_table, precision=highest)
    turned = jnp.einsum("kajm,al->lkjm", blocks, sine_table, precision=highest)
    return combine(plain_part, turned, orientation).reshape(length, 2, width_cols)


def centered_wave(index_of, length):
    shifted = jnp.where(index_of < length // 2, index_of, index_of - length)
    return shifted.astype(jnp.float32) * (2.0 * math.pi / length)


def forward_rows(loaded, mode_count, groups):
    lateral = loaded.shape[2]
    local_modes = mode_count // groups
    cosine_table, sine_table = dft_table(lateral, mode_count, lateral)
    cos_blocks = cosine_table.reshape(lateral, groups, local_modes)
    sin_blocks = sine_table.reshape(lateral, groups, local_modes)
    real_part = jnp.einsum("zxy,ygk->gxzk", loaded, cos_blocks, precision=highest)
    imag_part = -jnp.einsum("zxy,ygk->gxzk", loaded, sin_blocks, precision=highest)
    return jnp.stack([real_part, imag_part], axis=2).reshape(groups, -1)


def fold_depth(received, mode_count, groups, width_cells, depth_cells):
    local_modes = mode_count // groups
    total_x = groups * width_cells
    columns = received.reshape(total_x, 2, depth_cells * local_modes)
    spectrum = transform(columns, -1.0).reshape(total_x, 2, depth_cells, local_modes)
    index_x = jnp.arange(total_x, dtype=jnp.int32)
    index_y = lax.axis_index("gx") * local_modes + jnp.arange(local_modes, dtype=jnp.int32)
    wave_x = centered_wave(index_x, total_x)
    wave_y = centered_wave(index_y, NY)
    magnitude = jnp.sqrt(wave_x[:, None] ** 2 + wave_y[None, :] ** 2)
    depth_of = (
        lax.axis_index("gz") * depth_cells + jnp.arange(depth_cells, dtype=jnp.int32)
    ).astype(jnp.float32)
    depth_of = (depth_of + 0.5) * layer_depth
    retained = (
        (index_y != NY // 2)[None, :]
        & jnp.logical_not((index_x == 0)[:, None] & (index_y == 0)[None, :])
    ).astype(jnp.float32)
    weights = (
        gravity_scale
        * layer_depth
        * jnp.exp(-magnitude[:, None, :] * depth_of[None, :, None])
        * retained[:, None, :]
    )
    partial_value = jnp.sum(weights[:, None] * spectrum, axis=2)
    summed = lax.psum(partial_value, "gz")
    restored = transform(summed, 1.0)
    return restored.reshape(groups, width_cells * 2 * local_modes)


def finish(returned, mode_count, groups, width_cells):
    local_modes = mode_count // groups
    columns = returned.reshape(groups, width_cells, 2, local_modes)
    mode_index = jnp.arange(mode_count, dtype=jnp.int32)
    factor = jnp.where(mode_index == 0, 1.0, 1.0)
    cosine_table, sine_table = dft_table(mode_count, NY, NY)
    cos_blocks = (factor[:, None] * cosine_table).reshape(groups, local_modes, NY)
    sin_blocks = (factor[:, None] * sine_table).reshape(groups, local_modes, NY)
    real_sum = jnp.einsum("sxk,sky->xy", columns[:, :, 0], cos_blocks, precision=highest)
    imag_sum = jnp.einsum("sxk,sky->xy", columns[:, :, 1], sin_blocks, precision=highest)
    return (real_sum - imag_sum) / (groups * width_cells * NY)


def body(phases, velocity, pressure, density_table, viscosity_table):
    classes = jnp.arange(density_table.shape[0], dtype=jnp.int32)[:, None, None, None]
    chosen = phases[None] == classes
    density = jnp.sum(jnp.where(chosen, density_table[:, None, None, None], 0.0), axis=0)
    viscosity = jnp.sum(jnp.where(chosen, viscosity_table[:, None, None, None], 0.0), axis=0)
    effective = 1.0 / (1.0 / viscosity + 1.0 / shear_time)
    depth_cells, width_cells, lateral = pressure.shape
    groups = lax.axis_size("gx")
    fields = jnp.concatenate([velocity, pressure[None]], axis=0)
    margin = ((1, 1), (1, 1), (0, 0))
    for sweeps in range(ITERS):
        stacked = jnp.concatenate([fields, effective[None]], axis=0)
        widened = with_halo(stacked, (("gx", 2), ("gz", 1)), 1)
        fields = relaxation(
            widened[:4], widened[4], jnp.pad(density, margin), jnp.pad(pressure, margin)
        )
    velocity_out = fields[:3]
    pressure_out = fields[3]
    loaded = density * (1.0 + squeeze * pressure_out)
    packed = forward_rows(loaded, lateral, groups)
    received = lax.all_to_all(packed, "gx", split_axis=0, concat_axis=0, tiled=True)
    folded = fold_depth(received, lateral, groups, width_cells, depth_cells)
    returned = lax.all_to_all(folded, "gx", split_axis=0, concat_axis=0, tiled=True)
    gravity = finish(returned, lateral, groups, width_cells)
    return (velocity_out, pressure_out, gravity)


HALF_MODES = NY // 2
MESH = pl.DeviceIdType.MESH


def split_table(table):
    high = table.astype(jnp.bfloat16)
    low = (table - high.astype(np.float32)).astype(jnp.bfloat16)
    return high, low


def host_tables(layers, width, total_x):
    y = np.arange(NY)[:, None]
    k = np.arange(HALF_MODES)[None, :]
    angle = (y * k % NY) * (2.0 * np.pi / NY)
    along_y = np.stack(
        [part.reshape(NY, layers, -1) for part in (np.cos(angle), -np.sin(angle))], axis=2
    ).reshape(NY, 2 * HALF_MODES).astype(np.float32)
    kx = np.arange(total_x)[:, None]
    local = np.arange(width)[None, :]
    angle = (kx * local % total_x) * (2.0 * np.pi / total_x)
    c, s = np.cos(angle), np.sin(angle)
    along_x = np.block([[c, s], [-s, c]]).astype(np.float32)
    high, low = split_table(along_x)
    along_x = np.concatenate([high, high, low], axis=1)
    x = np.arange(total_x)[None, :]
    angle = (kx * x % total_x) * (2.0 * np.pi / total_x)
    c, s = np.cos(angle), np.sin(angle)
    back_x = np.block([[c, -s], [s, c]]).astype(np.float32)
    return np.stack(split_table(along_y)), along_x, np.stack(split_table(back_x))


def split_value(value):
    high = value.astype(jnp.bfloat16)
    low = (value - high.astype(jnp.float32)).astype(jnp.bfloat16)
    return high, low


def dot(left, right):
    return jnp.dot(left, right, preferred_element_type=jnp.float32)


def dot_turned(left, right):
    return lax.dot_general(
        left, right, (((1,), (1,)), ((), ())), preferred_element_type=jnp.float32
    )


def wave_of(index, length):
    shifted = jnp.where(index < length // 2, index, index - length)
    return shifted.astype(jnp.float32) * (2.0 * math.pi / length)


def new_velocity(f, value, side, faces, gradient, density, inverse):
    flux = faces[0] * side[0]
    for n in range(1, 6):
        flux = flux + faces[n] * side[n]
    forcing = flux - sum(faces[1:], faces[0]) * value - gradient
    if f == 2:
        forcing = forcing - 2.0 * density
    return value + (0.5 * velocity_rate) * inverse * forcing


def new_pressure(value, spread, start):
    return value - pressure_rate * (0.5 * spread + (value - start) / bulk_time)


def beside_y(tile):
    lateral = tile.shape[1]
    lane = lax.broadcasted_iota(jnp.int32, tile.shape, 1)
    return (
        jnp.where(lane == lateral - 1, 0.0, pltpu.roll(tile, lateral - 1, 1)),
        jnp.where(lane == 0, 0.0, pltpu.roll(tile, 1, 1)),
    )


def beside_plane(ref, lead, z):
    plane = ref[lead + (z + 1,)]
    width = plane.shape[0]
    ahead, behind = beside_y(plane)
    return plane, (
        pltpu.roll(plane, width - 1, 0), pltpu.roll(plane, 1, 0), ahead, behind,
        ref[lead + (z + 2,)], ref[lead + (z,)],
    )


def inner_velocity(z, block, eta, density, inverse):
    center, others = beside_plane(eta, (), z)
    faces = [center + other for other in others]
    pairs = [beside_plane(block, (f,), z) for f in range(4)]
    push = pairs[3][1]
    return [
        new_velocity(
            f, pairs[f][0], pairs[f][1], faces, push[2 * f] - push[2 * f + 1], density[z], inverse[z]
        )
        for f in range(3)
    ]


def inner_pressure(z, block, start):
    width = block.shape[2]
    along_x, along_y = block[0, z + 1], block[1, z + 1]
    ahead, behind = beside_y(along_y)
    spread = pltpu.roll(along_x, width - 1, 0) - pltpu.roll(along_x, 1, 0)
    spread = spread + (ahead - behind) + (block[2, z + 2] - block[2, z])
    return new_pressure(block[3, z + 1], spread, start[3, z + 1])


def beside_row(ref, lead, row, outer):
    depth = ref.shape[-3] - 2
    tile = ref[lead + (slice(1, depth + 1), row)]
    layer = lax.broadcasted_iota(jnp.int32, tile.shape, 0)
    below = jnp.where(layer == 0, ref[lead + (slice(0, 1), row)], pltpu.roll(tile, 1, 0))
    above = jnp.where(
        layer == depth - 1,
        ref[lead + (slice(depth + 1, depth + 2), row)],
        pltpu.roll(tile, depth - 1, 0),
    )
    ahead, behind = beside_y(tile)
    inner = ref[lead + (slice(1, depth + 1), row + 1 if row == 0 else row - 1)]
    along = (inner, outer) if row == 0 else (outer, inner)
    return tile, along + (ahead, behind, above, below)


def edge_velocity(wanted, row, block, eta, halo, eta_halo, density, inverse):
    center, others = beside_row(eta, (), row, eta_halo[...])
    faces = [center + other for other in others]
    push = beside_row(block, (3,), row, halo[3])[1]
    results = []
    for f in wanted:
        value, side = beside_row(block, (f,), row, halo[f])
        results.append(
            new_velocity(
                f, value, side, faces, push[2 * f] - push[2 * f + 1], density[:, row],
                inverse[:, row],
            )
        )
    return results


def edge_pressure(row, block, halo, start):
    depth = block.shape[1] - 2
    spread = None
    for f in range(3):
        side = beside_row(block, (f,), row, halo[f])[1]
        change = side[2 * f] - side[2 * f + 1]
        spread = change if spread is None else spread + change
    here = slice(1, depth + 1)
    return new_pressure(block[3, here, row], spread, start[3, here, row])


def kernel(
    groups, layers,
    dens_ref, visc_ref, phases_hbm, velocity_hbm, pressure_hbm,
    ty_hbm, along_x_hbm, bx_hbm,
    result, waves_out,
    ph, fields, eta, middle, density, inverse,
    send_low, send_high, get_low, get_high, send_low2, send_high2, get_low2, get_high2,
    eta_send_low, eta_send_high, eta_low, eta_high,
    ty, along_x, bx,
    loaded, partial, got_z, mine, got_x, whole,
    load_sem, z_sem, x_sem, pair_sem, send_sem, recv_sem,
):
    model, gx, gz = lax.axis_index("models"), lax.axis_index("gx"), lax.axis_index("gz")
    depth, width, lateral = density.shape
    total_x = groups * width
    last = width - 1

    loads = [
        pltpu.make_async_copy(src, dst, load_sem.at[i])
        for i, (src, dst) in enumerate(
            [
                (velocity_hbm, fields.at[pl.ds(0, 3), pl.ds(1, depth)]),
                (pressure_hbm, fields.at[3, pl.ds(1, depth)]),
                (phases_hbm, ph),
                (ty_hbm, ty),
                (along_x_hbm, along_x),
                (bx_hbm, bx),
            ]
        )
    ]
    for copy in loads[:3]:
        copy.start()

    barrier = pltpu.get_barrier_semaphore()
    partners = [(lax.rem(gx + j, groups), gz) for j in range(1, groups)] + [(gx, 1 - gz)]
    for other_x, other_z in partners:
        pl.semaphore_signal(
            barrier, inc=1, device_id=(model, other_x, other_z), device_id_type=MESH
        )

    edge = (depth + 1) * gz
    empty = jnp.zeros((width, lateral), jnp.float32)
    eta[edge] = empty
    for f in range(4):
        fields[f, edge] = empty
        middle[f, edge] = empty

    @pl.when(gx == 0)
    def _():
        for ref in (get_low, get_low2, eta_low):
            ref[...] = jnp.zeros_like(ref)

    @pl.when(gx == groups - 1)
    def _():
        for ref in (get_high, get_high2, eta_high):
            ref[...] = jnp.zeros_like(ref)

    def beside_x(stage, out_low, out_high, in_low, in_high):
        down = pltpu.make_async_remote_copy(
            src_ref=out_low, dst_ref=in_high,
            send_sem=x_sem.at[4 * stage], recv_sem=x_sem.at[4 * stage + 1],
            device_id=(model, lax.rem(gx + groups - 1, groups), gz), device_id_type=MESH,
        )
        up = pltpu.make_async_remote_copy(
            src_ref=out_high, dst_ref=in_low,
            send_sem=x_sem.at[4 * stage + 2], recv_sem=x_sem.at[4 * stage + 3],
            device_id=(model, lax.rem(gx + 1, groups), gz), device_id_type=MESH,
        )
        return down, up

    def send(pairs, rows=(0, last)):
        if 0 in rows:
            @pl.when(gx > 0)
            def _():
                for down, up in pairs:
                    down.start()

        if last in rows:
            @pl.when(gx < groups - 1)
            def _():
                for down, up in pairs:
                    up.start()

    def receive(pairs, row):
        if row == 0:
            @pl.when(gx > 0)
            def _():
                for down, up in pairs:
                    up.wait_recv()
        else:
            @pl.when(gx < groups - 1)
            def _():
                for down, up in pairs:
                    down.wait_recv()

    def all_sent(pairs):
        @pl.when(gx > 0)
        def _():
            for down, up in pairs:
                down.wait_send()

        @pl.when(gx < groups - 1)
        def _():
            for down, up in pairs:
                up.wait_send()

    def beside_z(stage, source, target):
        copy = pltpu.make_async_remote_copy(
            src_ref=source, dst_ref=target,
            send_sem=z_sem.at[2 * stage], recv_sem=z_sem.at[2 * stage + 1],
            device_id=(model, gx, 1 - gz), device_id_type=MESH,
        )
        copy.start()
        return copy

    bundle = (send_low, send_high, get_low, get_high)
    bundle2 = (send_low2, send_high2, get_low2, get_high2)
    x_u = beside_x(0, *[ref.at[0] for ref in bundle])
    x_p = beside_x(1, *[ref.at[3] for ref in bundle])
    x_eta = beside_x(2, eta_send_low, eta_send_high, eta_low, eta_high)
    x_rest = beside_x(3, *[ref.at[pl.ds(1, 2)] for ref in bundle])
    x_u2 = beside_x(4, *[ref.at[0] for ref in bundle2])
    x_rest2 = beside_x(5, *[ref.at[pl.ds(1, 3)] for ref in bundle2])
    edges = (
        (0, get_low, eta_low, send_low2, get_low2),
        (last, get_high, eta_high, send_high2, get_high2),
    )

    facing = depth - (depth - 1) * gz
    loads[0].wait()
    loads[1].wait()
    for f in range(4):
        send_low[f] = fields[f, 1 : depth + 1, 0]
        send_high[f] = fields[f, 1 : depth + 1, last]
    pl.semaphore_wait(barrier, len(partners))
    send([x_u, x_p])
    z_first = beside_z(0, fields.at[:, facing], fields.at[:, edge])

    loads[2].wait()
    for copy in loads[3:]:
        copy.start()

    def look_up(z, carry):
        kind = ph[z]
        dens = jnp.full(kind.shape, dens_ref[0], jnp.float32)
        visc = jnp.full(kind.shape, visc_ref[0], jnp.float32)
        for c in range(1, dens_ref.shape[0]):
            here = kind == c
            dens = jnp.where(here, dens_ref[c], dens)
            visc = jnp.where(here, visc_ref[c], visc)
        inv = 1.0 / visc + 1.0 / shear_time
        density[z] = dens
        inverse[z] = inv
        eta[z + 1] = 1.0 / inv
        return carry

    lax.fori_loop(0, depth, look_up, 0)
    eta_send_low[...] = eta[1 : depth + 1, 0]
    eta_send_high[...] = eta[1 : depth + 1, last]
    send([x_eta, x_rest])
    z_eta = beside_z(1, eta.at[facing], eta.at[edge])
    z_first.wait()
    z_eta.wait()

    def first(z, carry):
        values = inner_velocity(z, fields, eta, density, inverse)
        for f in range(3):
            middle[f, z + 1] = values[f]
        middle[3, z + 1] = inner_pressure(z, fields, fields)
        return carry

    lax.fori_loop(0, depth, first, 0)

    for row, halo, eta_halo, out, later in edges:
        receive([x_u, x_p, x_eta], row)
        out[0] = edge_velocity((0,), row, fields, eta, halo, eta_halo, density, inverse)[0]
        send([x_u2], (row,))
    for row, halo, eta_halo, out, later in edges:
        receive([x_rest], row)
        out[1], out[2] = edge_velocity(
            (1, 2), row, fields, eta, halo, eta_halo, density, inverse
        )
        out[3] = edge_pressure(row, fields, halo, fields)
    for row, halo, eta_halo, out, later in edges:
        for f in range(4):
            middle[f, 1 : depth + 1, row] = out[f]
    z_second = beside_z(2, middle.at[:, facing], middle.at[:, edge])
    send([x_rest2])
    z_second.wait()

    def second(z, carry):
        pressure = inner_pressure(z, middle, fields)
        result[3, z] = pressure
        loaded[z] = density[z] * (1.0 + squeeze * pressure)
        return carry

    lax.fori_loop(0, depth, second, 0)

    index_x = lax.broadcasted_iota(jnp.int32, (total_x, HALF_MODES), 0)
    index_y = lax.broadcasted_iota(jnp.int32, (total_x, HALF_MODES), 1)
    wx, wy = wave_of(index_x, total_x), wave_of(index_y, NY)
    magnitude = jnp.sqrt(wx * wx + wy * wy)
    decay = jnp.exp(-layer_depth * magnitude)
    top = layer_depth * (0.5 + depth * gz.astype(jnp.float32))
    scale = gravity_scale * layer_depth / (total_x * NY)
    weight = scale * jnp.exp(-top * magnitude)
    weight = weight * jnp.where(index_y == 0, jnp.where(index_x == 0, 0.0, 1.0), 2.0)
    for copy in loads[3:]:
        copy.wait()
    for row, halo, eta_halo, out, later in edges:
        receive([x_u2], row)
        pressure = edge_pressure(row, middle, later, fields)
        result[3, :, row] = pressure
        loaded[:, row] = density[:, row] * (1.0 + squeeze * pressure)

    high, low = split_value(loaded[...].reshape(depth * width, lateral))
    both = dot(jnp.concatenate([high, low], axis=0), ty[0])
    rows = both[: depth * width] + both[depth * width :] + dot(high, ty[1])
    held = HALF_MODES // layers
    parts = [rows[:, held * i : held * (i + 1)] for i in range(2 * layers)]
    real = jnp.concatenate(parts[0::2], axis=1)
    imag = jnp.concatenate(parts[1::2], axis=1)
    decay = jnp.concatenate([decay, decay], axis=0)
    weights = along_x[...]
    total = None
    for z in range(depth - 1, -1, -1):
        here = slice(z * width, (z + 1) * width)
        layer = jnp.concatenate([real[here], imag[here]], axis=0)
        high, low = split_value(layer)
        spectrum = dot(weights, jnp.concatenate([high, low, high], axis=0))
        total = spectrum if total is None else total * decay + spectrum

    high, low = split_value(total * jnp.concatenate([weight, weight], axis=0))
    both = dot(bx[0], jnp.concatenate([high, low], axis=1))
    field = both[:, :HALF_MODES] + both[:, HALF_MODES:] + dot(bx[1], high)
    for i in range(layers):
        partial[i] = field[:, held * i : held * (i + 1)].reshape(2, groups, width, held)

    near = groups // 4
    spans = [(near, groups - 2 * near), (0, near), (groups - near, near)]
    across = []
    for i, (begin, count) in enumerate(spans):
        block = pl.ds(begin, count)
        copy = pltpu.make_async_remote_copy(
            src_ref=partial.at[1 - gz, :, block],
            dst_ref=got_z.at[:, block],
            send_sem=pair_sem.at[2 * i], recv_sem=pair_sem.at[2 * i + 1],
            device_id=(model, gx, 1 - gz), device_id_type=MESH,
        )
        copy.start()
        across.append(copy)
    copies = []
    for (begin, count), arrival in zip(spans, across):
        block = pl.ds(begin, count)
        arrival.wait_recv()
        mine[:, block] = partial[gz, :, block] + got_z[:, block]
        offsets = range(max(begin, 1), begin + count)
        for j in sorted(offsets, key=lambda j: -min(j, groups - j)):
            copy = pltpu.make_async_remote_copy(
                src_ref=mine.at[:, j],
                dst_ref=got_x.at[j],
                send_sem=send_sem.at[j], recv_sem=recv_sem.at[j],
                device_id=(model, lax.rem(gx + j, groups), gz), device_id_type=MESH,
            )
            copy.start()
            copies.append((j, copy))

    def third(z, carry):
        values = inner_velocity(z, middle, eta, density, inverse)
        for f in range(3):
            result[f, z] = values[f]
        return carry

    lax.fori_loop(0, depth, third, 0)
    for row, halo, eta_halo, out, later in edges:
        receive([x_rest2], row)
        values = edge_velocity((0, 1, 2), row, middle, eta, later, eta_halo, density, inverse)
        for f in range(3):
            result[f, :, row] = values[f]
    all_sent([x_u, x_p, x_eta, x_rest, x_u2, x_rest2])

    summed = mine[:, 0]
    for j, copy in copies:
        copy.wait_recv()
        summed = summed + got_x[j]
    whole[gz] = summed
    last_copy = pltpu.make_async_remote_copy(
        src_ref=whole.at[gz], dst_ref=whole.at[gz],
        send_sem=pair_sem.at[6], recv_sem=pair_sem.at[7],
        device_id=(model, gx, 1 - gz), device_id_type=MESH,
    )
    last_copy.start()
    for j, copy in copies:
        copy.wait_send()
    for copy in across:
        copy.wait_send()
    last_copy.wait()
    waves_out[...] = jnp.concatenate(
        [whole[i, part] for i in range(layers) for part in range(2)], axis=1
    )


def last_kernel(result, waves, ty, velocity_out, pressure_out, gravity, sem):
    outs = [
        pltpu.make_async_copy(result.at[pl.ds(0, 3)], velocity_out, sem.at[0]),
        pltpu.make_async_copy(result.at[3], pressure_out, sem.at[1]),
    ]
    for copy in outs:
        copy.start()
    width = waves.shape[0]
    high, low = split_value(waves[...])
    both = dot_turned(jnp.concatenate([high, low], axis=0), ty[0])
    gravity[...] = both[:width] + both[width:] + dot_turned(high, ty[1])
    for copy in outs:
        copy.wait()


def fused_body(phases, velocity, pressure, density_table, viscosity_table):
    depth, width, lateral = pressure.shape
    groups, layers = lax.axis_size("gx"), lax.axis_size("gz")
    total_x = groups * width
    ty, along_x, bx = host_tables(layers, width, total_x)
    held = HALF_MODES // layers
    shares = pltpu.VMEM((2, groups, width, held), jnp.float32)
    f32, b16 = jnp.float32, jnp.bfloat16
    vmem = pl.BlockSpec(memory_space=pltpu.VMEM)
    smem = pl.BlockSpec(memory_space=pltpu.SMEM)
    hbm = pl.BlockSpec(memory_space=pltpu.HBM)
    rows = pltpu.VMEM((4, depth, lateral), f32)
    eta_rows = pltpu.VMEM((depth, lateral), f32)
    cells = (depth, width, lateral)
    sems = pltpu.SemaphoreType.DMA
    along_y = jnp.asarray(ty)
    result, waves = pl.pallas_call(
        functools.partial(kernel, groups, layers),
        out_shape=(
            pltpu.VMEM((4,) + cells, f32),
            pltpu.VMEM((width, 2 * HALF_MODES), f32),
        ),
        in_specs=[smem, smem] + [hbm] * 6,
        out_specs=(vmem, vmem),
        scratch_shapes=[
            pltpu.VMEM(cells, jnp.int32),
            pltpu.VMEM((4, depth + 2, width, lateral), f32),
            pltpu.VMEM((depth + 2, width, lateral), f32),
            pltpu.VMEM((4, depth + 2, width, lateral), f32),
            pltpu.VMEM(cells, f32),
            pltpu.VMEM(cells, f32),
            rows, rows, rows, rows, rows, rows, rows, rows,
            eta_rows, eta_rows, eta_rows, eta_rows,
            pltpu.VMEM(ty.shape, b16),
            pltpu.VMEM(along_x.shape, b16),
            pltpu.VMEM(bx.shape, b16),
            pltpu.VMEM(cells, f32),
            pltpu.VMEM((layers, 2, groups, width, held), f32),
            shares, shares,
            pltpu.VMEM((groups, 2, width, held), f32),
            pltpu.VMEM((layers, 2, width, held), f32),
            sems((6,)), sems((6,)), sems((24,)), sems((8,)),
            sems((groups,)), sems((groups,)),
        ],
        compiler_params=pltpu.CompilerParams(
            collective_id=0, has_side_effects=True, vmem_limit_bytes=56 * 1024 * 1024
        ),
    )(
        density_table, viscosity_table, phases, velocity, pressure,
        along_y, jnp.asarray(along_x), jnp.asarray(bx),
    )
    return pl.pallas_call(
        last_kernel,
        out_shape=(
            jax.ShapeDtypeStruct(velocity.shape, f32),
            jax.ShapeDtypeStruct(pressure.shape, f32),
            jax.ShapeDtypeStruct((width, lateral), f32),
        ),
        in_specs=[vmem] * 3,
        out_specs=(hbm, hbm, vmem),
        scratch_shapes=[sems((2,))],
        compiler_params=pltpu.CompilerParams(vmem_limit_bytes=16 * 1024 * 1024),
    )(result, waves, along_y)


def local_program(phases, velocity, pressure, density_table, viscosity_table):
    depth, width, lateral = pressure.shape
    groups, layers = lax.axis_size("gx"), lax.axis_size("gz")
    fits = layers == 2 and groups * width == 128 and width == 16 and depth % 8 == 0
    chosen = fused_body if fits else body
    return chosen(phases, velocity, pressure, density_table, viscosity_table)


def solution(mesh):
    in_specs = (
        P(("models", "gz"), "gx", None),
        P(None, ("models", "gz"), "gx", None),
        P(("models", "gz"), "gx", None),
        P(),
        P(),
    )
    out_specs = (
        P(None, ("models", "gz"), "gx", None),
        P(("models", "gz"), "gx", None),
        P(("models", "gx"), None),
    )
    return jax.shard_map(local_program, mesh=mesh, in_specs=in_specs, out_specs=out_specs, check_vma=False)
```

```python
import functools
import math

import jax
import jax.numpy as jnp
import numpy as np
from jax import lax
from jax.experimental import pallas as pl
from jax.experimental.pallas import tpu as pltpu
from jax.sharding import PartitionSpec as P

NY = 512
ITERS = 2


velocity_rate = 0.1
pressure_rate = 0.5
bulk_time = 2.0
shear_time = 4.0
squeeze = 0.25
gravity_scale = 4.0
layer_depth = 0.125
highest = lax.Precision.HIGHEST


def with_halo(block, sides, width):
    for axis, dim in sides:
        count = lax.axis_size(axis)
        forward = [(i, i + 1) for i in range(count - 1)]
        backward = [(target, source) for source, target in forward]
        low = lax.ppermute(
            lax.slice_in_dim(block, block.shape[dim] - width, None, axis=dim), axis, forward
        )
        high = lax.ppermute(lax.slice_in_dim(block, 0, width, axis=dim), axis, backward)
        block = jnp.concatenate([low, block, high], axis=dim)
    return block


def neighbour(field, dim_index, offset):
    lead_count = field.ndim - 3
    pieces = [slice(None)] * lead_count + [slice(1, -1), slice(1, -1), slice(1, -1)]
    pieces[lead_count + dim_index] = slice(2, None) if offset > 0 else slice(0, -2)
    return field[tuple(pieces)]


def center(field):
    lead_count = field.ndim - 3
    pieces = [slice(None)] * lead_count + [slice(1, -1), slice(1, -1), slice(1, -1)]
    return field[tuple(pieces)]


def relaxation(fields, viscous, density, previous):
    padded = jnp.pad(fields, ((0, 0), (0, 0), (0, 0), (1, 1)))
    eta_full = jnp.pad(viscous, ((0, 0), (0, 0), (1, 1)))
    eta_core = center(eta_full)
    pressure_full = padded[3]
    results = []
    for component, dim_index in ((0, 1), (1, 2), (2, 0)):
        moving = padded[component]
        moving_core = center(moving)
        stress = jnp.zeros_like(moving_core)
        for facing in range(3):
            for offset in (1, -1):
                face_eta = 0.5 * (eta_core + neighbour(eta_full, facing, offset))
                stress = stress + face_eta * (neighbour(moving, facing, offset) - moving_core)
        forcing = stress - 0.5 * (
            neighbour(pressure_full, dim_index, 1) - neighbour(pressure_full, dim_index, -1)
        )
        if component == 2:
            forcing = forcing - density[1:-1, 1:-1, :]
        results.append(moving_core + velocity_rate * forcing / eta_core)
    spread = jnp.zeros_like(eta_core)
    for component, dim_index in ((0, 1), (1, 2), (2, 0)):
        spread = spread + 0.5 * (
            neighbour(padded[component], dim_index, 1) - neighbour(padded[component], dim_index, -1)
        )
    pressure_core = center(pressure_full)
    results.append(
        pressure_core
        - pressure_rate * (spread + (pressure_core - previous[1:-1, 1:-1, :]) / bulk_time)
    )
    return jnp.stack(results)


def dft_table(row_count, col_count, period):
    row_index = jnp.arange(row_count, dtype=jnp.int32)[:, None]
    col_index = jnp.arange(col_count, dtype=jnp.int32)[None, :]
    angles = (row_index * col_index % period).astype(jnp.float32) * (2.0 * math.pi / period)
    return (jnp.cos(angles), jnp.sin(angles))


def combine(plain_part, turned, orientation):
    real_part = plain_part[:, :, 0] - orientation * turned[:, :, 1]
    imag_part = plain_part[:, :, 1] + orientation * turned[:, :, 0]
    return jnp.stack([real_part, imag_part], axis=2)


def transform(columns, orientation):
    length = columns.shape[0]
    width_cols = columns.shape[2]
    inner_size = math.gcd(length, 128)
    outer_size = length // inner_size
    blocks = columns.reshape(inner_size, outer_size, 2, width_cols)
    cosine_table, sine_table = dft_table(inner_size, inner_size, inner_size)
    plain_part = jnp.einsum("bajm,bk->kajm", blocks, cosine_table, precision=highest)
    turned = jnp.einsum("bajm,bk->kajm", blocks, sine_table, precision=highest)
    blocks = combine(plain_part, turned, orientation)
    twist_cos, twist_sin = dft_table(inner_size, outer_size, length)
    twist_cos = twist_cos[:, :, None]
    twist_sin = twist_sin[:, :, None]
    real_part = blocks[:, :, 0]
    imag_part = blocks[:, :, 1]
    blocks = jnp.stack(
        [
            real_part * twist_cos - orientation * imag_part * twist_sin,
            imag_part * twist_cos + orientation * real_part * twist_sin,
        ],
        axis=2,
    )
    cosine_table, sine_table = dft_table(outer_size, outer_size, outer_size)
    plain_part = jnp.einsum("kajm,al->lkjm", blocks, cosine_table, precision=highest)
    turned = jnp.einsum("kajm,al->lkjm", blocks, sine_table, precision=highest)
    return combine(plain_part, turned, orientation).reshape(length, 2, width_cols)


def centered_wave(index_of, length):
    shifted = jnp.where(index_of < length // 2, index_of, index_of - length)
    return shifted.astype(jnp.float32) * (2.0 * math.pi / length)


def forward_rows(loaded, mode_count, groups):
    lateral = loaded.shape[2]
    local_modes = mode_count // groups
    cosine_table, sine_table = dft_table(lateral, mode_count, lateral)
    cos_blocks = cosine_table.reshape(lateral, groups, local_modes)
    sin_blocks = sine_table.reshape(lateral, groups, local_modes)
    real_part = jnp.einsum("zxy,ygk->gxzk", loaded, cos_blocks, precision=highest)
    imag_part = -jnp.einsum("zxy,ygk->gxzk", loaded, sin_blocks, precision=highest)
    return jnp.stack([real_part, imag_part], axis=2).reshape(groups, -1)


def fold_depth(received, mode_count, groups, width_cells, depth_cells):
    local_modes = mode_count // groups
    total_x = groups * width_cells
    columns = received.reshape(total_x, 2, depth_cells * local_modes)
    spectrum = transform(columns, -1.0).reshape(total_x, 2, depth_cells, local_modes)
    index_x = jnp.arange(total_x, dtype=jnp.int32)
    index_y = lax.axis_index("gx") * local_modes + jnp.arange(local_modes, dtype=jnp.int32)
    wave_x = centered_wave(index_x, total_x)
    wave_y = centered_wave(index_y, NY)
    magnitude = jnp.sqrt(wave_x[:, None] ** 2 + wave_y[None, :] ** 2)
    depth_of = (
        lax.axis_index("gz") * depth_cells + jnp.arange(depth_cells, dtype=jnp.int32)
    ).astype(jnp.float32)
    depth_of = (depth_of + 0.5) * layer_depth
    retained = (
        (index_y != NY // 2)[None, :]
        & jnp.logical_not((index_x == 0)[:, None] & (index_y == 0)[None, :])
    ).astype(jnp.float32)
    weights = (
        gravity_scale
        * layer_depth
        * jnp.exp(-magnitude[:, None, :] * depth_of[None, :, None])
        * retained[:, None, :]
    )
    partial_value = jnp.sum(weights[:, None] * spectrum, axis=2)
    summed = lax.psum(partial_value, "gz")
    restored = transform(summed, 1.0)
    return restored.reshape(groups, width_cells * 2 * local_modes)


def finish(returned, mode_count, groups, width_cells):
    local_modes = mode_count // groups
    columns = returned.reshape(groups, width_cells, 2, local_modes)
    mode_index = jnp.arange(mode_count, dtype=jnp.int32)
    factor = jnp.where(mode_index == 0, 1.0, 1.0)
    cosine_table, sine_table = dft_table(mode_count, NY, NY)
    cos_blocks = (factor[:, None] * cosine_table).reshape(groups, local_modes, NY)
    sin_blocks = (factor[:, None] * sine_table).reshape(groups, local_modes, NY)
    real_sum = jnp.einsum("sxk,sky->xy", columns[:, :, 0], cos_blocks, precision=highest)
    imag_sum = jnp.einsum("sxk,sky->xy", columns[:, :, 1], sin_blocks, precision=highest)
    return (real_sum - imag_sum) / (groups * width_cells * NY)


def body(phases, velocity, pressure, density_table, viscosity_table):
    classes = jnp.arange(density_table.shape[0], dtype=jnp.int32)[:, None, None, None]
    chosen = phases[None] == classes
    density = jnp.sum(jnp.where(chosen, density_table[:, None, None, None], 0.0), axis=0)
    viscosity = jnp.sum(jnp.where(chosen, viscosity_table[:, None, None, None], 0.0), axis=0)
    effective = 1.0 / (1.0 / viscosity + 1.0 / shear_time)
    depth_cells, width_cells, lateral = pressure.shape
    groups = lax.axis_size("gx")
    fields = jnp.concatenate([velocity, pressure[None]], axis=0)
    margin = ((1, 1), (1, 1), (0, 0))
    for sweeps in range(ITERS):
        stacked = jnp.concatenate([fields, effective[None]], axis=0)
        widened = with_halo(stacked, (("gx", 2), ("gz", 1)), 1)
        fields = relaxation(
            widened[:4], widened[4], jnp.pad(density, margin), jnp.pad(pressure, margin)
        )
    velocity_out = fields[:3]
    pressure_out = fields[3]
    loaded = density * (1.0 + squeeze * pressure_out)
    packed = forward_rows(loaded, lateral, groups)
    received = lax.all_to_all(packed, "gx", split_axis=0, concat_axis=0, tiled=True)
    folded = fold_depth(received, lateral, groups, width_cells, depth_cells)
    returned = lax.all_to_all(folded, "gx", split_axis=0, concat_axis=0, tiled=True)
    gravity = finish(returned, lateral, groups, width_cells)
    return (velocity_out, pressure_out, gravity)


HALF_MODES = NY // 2
MESH = pl.DeviceIdType.MESH


def split_table(table):
    high = table.astype(jnp.bfloat16)
    low = (table - high.astype(np.float32)).astype(jnp.bfloat16)
    return high, low


def host_tables(layers, width, total_x):
    y = np.arange(NY)[:, None]
    k = np.arange(HALF_MODES)[None, :]
    angle = (y * k % NY) * (2.0 * np.pi / NY)
    along_y = np.stack(
        [part.reshape(NY, layers, -1) for part in (np.cos(angle), -np.sin(angle))], axis=2
    ).reshape(NY, 2 * HALF_MODES).astype(np.float32)
    kx = np.arange(total_x)[:, None]
    local = np.arange(width)[None, :]
    angle = (kx * local % total_x) * (2.0 * np.pi / total_x)
    c, s = np.cos(angle), np.sin(angle)
    along_x = np.block([[c, s], [-s, c]]).astype(np.float32)
    high, low = split_table(along_x)
    along_x = np.concatenate([high, high, low], axis=1)
    x = np.arange(total_x)[None, :]
    angle = (kx * x % total_x) * (2.0 * np.pi / total_x)
    c, s = np.cos(angle), np.sin(angle)
    back_x = np.block([[c, -s], [s, c]]).astype(np.float32)
    return np.stack(split_table(along_y)), along_x, np.stack(split_table(back_x))


def split_value(value):
    high = value.astype(jnp.bfloat16)
    low = (value - high.astype(jnp.float32)).astype(jnp.bfloat16)
    return high, low


def dot(left, right):
    return jnp.dot(left, right, preferred_element_type=jnp.float32)


def dot_turned(left, right):
    return lax.dot_general(
        left, right, (((1,), (1,)), ((), ())), preferred_element_type=jnp.float32
    )


def wave_of(index, length):
    shifted = jnp.where(index < length // 2, index, index - length)
    return shifted.astype(jnp.float32) * (2.0 * math.pi / length)


def new_velocity(f, value, side, faces, gradient, density, inverse):
    flux = faces[0] * side[0]
    for n in range(1, 6):
        flux = flux + faces[n] * side[n]
    forcing = flux - sum(faces[1:], faces[0]) * value - gradient
    if f == 2:
        forcing = forcing - 2.0 * density
    return value + (0.5 * velocity_rate) * inverse * forcing


def new_pressure(value, spread, start):
    return value - pressure_rate * (0.5 * spread + (value - start) / bulk_time)


def beside_y(tile):
    lateral = tile.shape[1]
    lane = lax.broadcasted_iota(jnp.int32, tile.shape, 1)
    return (
        jnp.where(lane == lateral - 1, 0.0, pltpu.roll(tile, lateral - 1, 1)),
        jnp.where(lane == 0, 0.0, pltpu.roll(tile, 1, 1)),
    )


def beside_plane(ref, lead, z):
    plane = ref[lead + (z + 1,)]
    width = plane.shape[0]
    ahead, behind = beside_y(plane)
    return plane, (
        pltpu.roll(plane, width - 1, 0), pltpu.roll(plane, 1, 0), ahead, behind,
        ref[lead + (z + 2,)], ref[lead + (z,)],
    )


def inner_velocity(z, block, eta, density, inverse):
    center, others = beside_plane(eta, (), z)
    faces = [center + other for other in others]
    pairs = [beside_plane(block, (f,), z) for f in range(4)]
    push = pairs[3][1]
    return [
        new_velocity(
            f, pairs[f][0], pairs[f][1], faces, push[2 * f] - push[2 * f + 1], density[z], inverse[z]
        )
        for f in range(3)
    ]


def inner_pressure(z, block, start):
    width = block.shape[2]
    along_x, along_y = block[0, z + 1], block[1, z + 1]
    ahead, behind = beside_y(along_y)
    spread = pltpu.roll(along_x, width - 1, 0) - pltpu.roll(along_x, 1, 0)
    spread = spread + (ahead - behind) + (block[2, z + 2] - block[2, z])
    return new_pressure(block[3, z + 1], spread, start[3, z + 1])


def beside_row(ref, lead, row, outer):
    depth = ref.shape[-3] - 2
    tile = ref[lead + (slice(1, depth + 1), row)]
    layer = lax.broadcasted_iota(jnp.int32, tile.shape, 0)
    below = jnp.where(layer == 0, ref[lead + (slice(0, 1), row)], pltpu.roll(tile, 1, 0))
    above = jnp.where(
        layer == depth - 1,
        ref[lead + (slice(depth + 1, depth + 2), row)],
        pltpu.roll(tile, depth - 1, 0),
    )
    ahead, behind = beside_y(tile)
    inner = ref[lead + (slice(1, depth + 1), row + 1 if row == 0 else row - 1)]
    along = (inner, outer) if row == 0 else (outer, inner)
    return tile, along + (ahead, behind, above, below)


def edge_velocity(wanted, row, block, eta, halo, eta_halo, density, inverse):
    center, others = beside_row(eta, (), row, eta_halo[...])
    faces = [center + other for other in others]
    push = beside_row(block, (3,), row, halo[3])[1]
    results = []
    for f in wanted:
        value, side = beside_row(block, (f,), row, halo[f])
        results.append(
            new_velocity(
                f, value, side, faces, push[2 * f] - push[2 * f + 1], density[:, row],
                inverse[:, row],
            )
        )
    return results


def edge_pressure(row, block, halo, start):
    depth = block.shape[1] - 2
    spread = None
    for f in range(3):
        side = beside_row(block, (f,), row, halo[f])[1]
        change = side[2 * f] - side[2 * f + 1]
        spread = change if spread is None else spread + change
    here = slice(1, depth + 1)
    return new_pressure(block[3, here, row], spread, start[3, here, row])


def kernel(
    groups, layers,
    dens_ref, visc_ref, phases_hbm, velocity_hbm, pressure_hbm,
    ty_hbm, along_x_hbm, bx_hbm,
    result, waves_out,
    ph, fields, eta, middle, density, inverse,
    send_low, send_high, get_low, get_high, send_low2, send_high2, get_low2, get_high2,
    eta_send_low, eta_send_high, eta_low, eta_high,
    ty, along_x, bx,
    loaded, partial, got_z, mine, got_x, whole,
    load_sem, z_sem, x_sem, pair_sem, send_sem, recv_sem,
):
    model, gx, gz = lax.axis_index("models"), lax.axis_index("gx"), lax.axis_index("gz")
    depth, width, lateral = density.shape
    total_x = groups * width
    last = width - 1

    loads = [
        pltpu.make_async_copy(src, dst, load_sem.at[i])
        for i, (src, dst) in enumerate(
            [
                (velocity_hbm, fields.at[pl.ds(0, 3), pl.ds(1, depth)]),
                (pressure_hbm, fields.at[3, pl.ds(1, depth)]),
                (phases_hbm, ph),
                (ty_hbm, ty),
                (along_x_hbm, along_x),
                (bx_hbm, bx),
            ]
        )
    ]
    for copy in loads[:3]:
        copy.start()

    barrier = pltpu.get_barrier_semaphore()
    partners = [(lax.rem(gx + j, groups), gz) for j in range(1, groups)] + [(gx, 1 - gz)]
    for other_x, other_z in partners:
        pl.semaphore_signal(
            barrier, inc=1, device_id=(model, other_x, other_z), device_id_type=MESH
        )

    edge = (depth + 1) * gz
    empty = jnp.zeros((width, lateral), jnp.float32)
    eta[edge] = empty
    for f in range(4):
        fields[f, edge] = empty
        middle[f, edge] = empty

    @pl.when(gx == 0)
    def _():
        for ref in (get_low, get_low2, eta_low):
            ref[...] = jnp.zeros_like(ref)

    @pl.when(gx == groups - 1)
    def _():
        for ref in (get_high, get_high2, eta_high):
            ref[...] = jnp.zeros_like(ref)

    def beside_x(stage, out_low, out_high, in_low, in_high):
        down = pltpu.make_async_remote_copy(
            src_ref=out_low, dst_ref=in_high,
            send_sem=x_sem.at[4 * stage], recv_sem=x_sem.at[4 * stage + 1],
            device_id=(model, lax.rem(gx + groups - 1, groups), gz), device_id_type=MESH,
        )
        up = pltpu.make_async_remote_copy(
            src_ref=out_high, dst_ref=in_low,
            send_sem=x_sem.at[4 * stage + 2], recv_sem=x_sem.at[4 * stage + 3],
            device_id=(model, lax.rem(gx + 1, groups), gz), device_id_type=MESH,
        )
        return down, up

    def send(pairs, rows=(0, last)):
        if 0 in rows:
            @pl.when(gx > 0)
            def _():
                for down, up in pairs:
                    down.start()

        if last in rows:
            @pl.when(gx < groups - 1)
            def _():
                for down, up in pairs:
                    up.start()

    def receive(pairs, row):
        if row == 0:
            @pl.when(gx > 0)
            def _():
                for down, up in pairs:
                    up.wait_recv()
        else:
            @pl.when(gx < groups - 1)
            def _():
                for down, up in pairs:
                    down.wait_recv()

    def all_sent(pairs):
        @pl.when(gx > 0)
        def _():
            for down, up in pairs:
                down.wait_send()

        @pl.when(gx < groups - 1)
        def _():
            for down, up in pairs:
                up.wait_send()

    def beside_z(stage, source, target):
        copy = pltpu.make_async_remote_copy(
            src_ref=source, dst_ref=target,
            send_sem=z_sem.at[2 * stage], recv_sem=z_sem.at[2 * stage + 1],
            device_id=(model, gx, 1 - gz), device_id_type=MESH,
        )
        copy.start()
        return copy

    bundle = (send_low, send_high, get_low, get_high)
    bundle2 = (send_low2, send_high2, get_low2, get_high2)
    x_u = beside_x(0, *[ref.at[0] for ref in bundle])
    x_p = beside_x(1, *[ref.at[3] for ref in bundle])
    x_eta = beside_x(2, eta_send_low, eta_send_high, eta_low, eta_high)
    x_rest = beside_x(3, *[ref.at[pl.ds(1, 2)] for ref in bundle])
    x_u2 = beside_x(4, *[ref.at[0] for ref in bundle2])
    x_rest2 = beside_x(5, *[ref.at[pl.ds(1, 3)] for ref in bundle2])
    edges = (
        (0, get_low, eta_low, send_low2, get_low2),
        (last, get_high, eta_high, send_high2, get_high2),
    )

    facing = depth - (depth - 1) * gz
    loads[0].wait()
    loads[1].wait()
    for f in range(4):
        send_low[f] = fields[f, 1 : depth + 1, 0]
        send_high[f] = fields[f, 1 : depth + 1, last]
    pl.semaphore_wait(barrier, len(partners))
    send([x_u, x_p])
    z_first = beside_z(0, fields.at[:, facing], fields.at[:, edge])

    loads[2].wait()
    for copy in loads[3:]:
        copy.start()

    def look_up(z, carry):
        kind = ph[z]
        dens = jnp.full(kind.shape, dens_ref[0], jnp.float32)
        visc = jnp.full(kind.shape, visc_ref[0], jnp.float32)
        for c in range(1, dens_ref.shape[0]):
            here = kind == c
            dens = jnp.where(here, dens_ref[c], dens)
            visc = jnp.where(here, visc_ref[c], visc)
        inv = 1.0 / visc + 1.0 / shear_time
        density[z] = dens
        inverse[z] = inv
        eta[z + 1] = 1.0 / inv
        return carry

    lax.fori_loop(0, depth, look_up, 0)
    eta_send_low[...] = eta[1 : depth + 1, 0]
    eta_send_high[...] = eta[1 : depth + 1, last]
    send([x_eta, x_rest])
    z_eta = beside_z(1, eta.at[facing], eta.at[edge])
    z_first.wait()
    z_eta.wait()

    def first(z, carry):
        values = inner_velocity(z, fields, eta, density, inverse)
        for f in range(3):
            middle[f, z + 1] = values[f]
        middle[3, z + 1] = inner_pressure(z, fields, fields)
        return carry

    lax.fori_loop(0, depth, first, 0)

    for row, halo, eta_halo, out, later in edges:
        receive([x_u, x_p, x_eta], row)
        out[0] = edge_velocity((0,), row, fields, eta, halo, eta_halo, density, inverse)[0]
        send([x_u2], (row,))
    for row, halo, eta_halo, out, later in edges:
        receive([x_rest], row)
        out[1], out[2] = edge_velocity(
            (1, 2), row, fields, eta, halo, eta_halo, density, inverse
        )
        out[3] = edge_pressure(row, fields, halo, fields)
    for row, halo, eta_halo, out, later in edges:
        for f in range(4):
            middle[f, 1 : depth + 1, row] = out[f]
    z_second = beside_z(2, middle.at[:, facing], middle.at[:, edge])
    send([x_rest2])
    z_second.wait()

    def second(z, carry):
        pressure = inner_pressure(z, middle, fields)
        result[3, z] = pressure
        loaded[z] = density[z] * (1.0 + squeeze * pressure)
        return carry

    lax.fori_loop(0, depth, second, 0)

    index_x = lax.broadcasted_iota(jnp.int32, (total_x, HALF_MODES), 0)
    index_y = lax.broadcasted_iota(jnp.int32, (total_x, HALF_MODES), 1)
    wx, wy = wave_of(index_x, total_x), wave_of(index_y, NY)
    magnitude = jnp.sqrt(wx * wx + wy * wy)
    decay = jnp.exp(-layer_depth * magnitude)
    top = layer_depth * (0.5 + depth * gz.astype(jnp.float32))
    scale = gravity_scale * layer_depth / (total_x * NY)
    weight = scale * jnp.exp(-top * magnitude)
    weight = weight * jnp.where(index_y == 0, jnp.where(index_x == 0, 0.0, 1.0), 2.0)
    for copy in loads[3:]:
        copy.wait()
    def along_y(value):
        count = value.shape[0]
        high, low = split_value(value)
        both = dot(jnp.concatenate([high, low], axis=0), ty[0])
        return both[:count] + both[count:] + dot(high, ty[1])

    loaded[...] = along_y(loaded[...].reshape(depth * width, lateral)).reshape(loaded.shape)
    edge_loads = []
    for row, halo, eta_halo, out, later in edges:
        receive([x_u2], row)
        pressure = edge_pressure(row, middle, later, fields)
        result[3, :, row] = pressure
        edge_loads.append(density[:, row] * (1.0 + squeeze * pressure))
    edge_modes = along_y(jnp.concatenate(edge_loads, axis=0))
    loaded[:, 0] = edge_modes[:depth]
    loaded[:, last] = edge_modes[depth:]

    rows = loaded[...].reshape(depth * width, 2 * HALF_MODES)
    held = HALF_MODES // layers
    parts = [rows[:, held * i : held * (i + 1)] for i in range(2 * layers)]
    real = jnp.concatenate(parts[0::2], axis=1)
    imag = jnp.concatenate(parts[1::2], axis=1)
    decay = jnp.concatenate([decay, decay], axis=0)
    weights = along_x[...]
    total = None
    for z in range(depth - 1, -1, -1):
        here = slice(z * width, (z + 1) * width)
        layer = jnp.concatenate([real[here], imag[here]], axis=0)
        high, low = split_value(layer)
        spectrum = dot(weights, jnp.concatenate([high, low, high], axis=0))
        total = spectrum if total is None else total * decay + spectrum

    high, low = split_value(total * jnp.concatenate([weight, weight], axis=0))
    both = dot(bx[0], jnp.concatenate([high, low], axis=1))
    field = both[:, :HALF_MODES] + both[:, HALF_MODES:] + dot(bx[1], high)
    for i in range(layers):
        partial[i] = field[:, held * i : held * (i + 1)].reshape(2, groups, width, held)

    near = groups // 4
    spans = [(near, groups - 2 * near), (0, near), (groups - near, near)]
    across = []
    for i, (begin, count) in enumerate(spans):
        block = pl.ds(begin, count)
        copy = pltpu.make_async_remote_copy(
            src_ref=partial.at[1 - gz, :, block],
            dst_ref=got_z.at[:, block],
            send_sem=pair_sem.at[2 * i], recv_sem=pair_sem.at[2 * i + 1],
            device_id=(model, gx, 1 - gz), device_id_type=MESH,
        )
        copy.start()
        across.append(copy)
    copies = []
    for (begin, count), arrival in zip(spans, across):
        block = pl.ds(begin, count)
        arrival.wait_recv()
        mine[:, block] = partial[gz, :, block] + got_z[:, block]
        offsets = range(max(begin, 1), begin + count)
        for j in sorted(offsets, key=lambda j: -min(j, groups - j)):
            copy = pltpu.make_async_remote_copy(
                src_ref=mine.at[:, j],
                dst_ref=got_x.at[j],
                send_sem=send_sem.at[j], recv_sem=recv_sem.at[j],
                device_id=(model, lax.rem(gx + j, groups), gz), device_id_type=MESH,
            )
            copy.start()
            copies.append((j, copy))

    def third(z, carry):
        values = inner_velocity(z, middle, eta, density, inverse)
        for f in range(3):
            result[f, z] = values[f]
        return carry

    lax.fori_loop(0, depth, third, 0)
    for row, halo, eta_halo, out, later in edges:
        receive([x_rest2], row)
        values = edge_velocity((0, 1, 2), row, middle, eta, later, eta_halo, density, inverse)
        for f in range(3):
            result[f, :, row] = values[f]
    all_sent([x_u, x_p, x_eta, x_rest, x_u2, x_rest2])

    summed = mine[:, 0]
    for j, copy in copies:
        copy.wait_recv()
        summed = summed + got_x[j]
    whole[gz] = summed
    last_copy = pltpu.make_async_remote_copy(
        src_ref=whole.at[gz], dst_ref=whole.at[gz],
        send_sem=pair_sem.at[6], recv_sem=pair_sem.at[7],
        device_id=(model, gx, 1 - gz), device_id_type=MESH,
    )
    last_copy.start()
    for j, copy in copies:
        copy.wait_send()
    for copy in across:
        copy.wait_send()
    last_copy.wait()
    waves_out[...] = jnp.concatenate(
        [whole[i, part] for i in range(layers) for part in range(2)], axis=1
    )


def last_kernel(result, waves, ty, velocity_out, pressure_out, gravity, sem):
    outs = [
        pltpu.make_async_copy(result.at[pl.ds(0, 3)], velocity_out, sem.at[0]),
        pltpu.make_async_copy(result.at[3], pressure_out, sem.at[1]),
    ]
    for copy in outs:
        copy.start()
    width = waves.shape[0]
    high, low = split_value(waves[...])
    both = dot_turned(jnp.concatenate([high, low], axis=0), ty[0])
    gravity[...] = both[:width] + both[width:] + dot_turned(high, ty[1])
    for copy in outs:
        copy.wait()


def fused_body(phases, velocity, pressure, density_table, viscosity_table):
    depth, width, lateral = pressure.shape
    groups, layers = lax.axis_size("gx"), lax.axis_size("gz")
    total_x = groups * width
    ty, along_x, bx = host_tables(layers, width, total_x)
    held = HALF_MODES // layers
    shares = pltpu.VMEM((2, groups, width, held), jnp.float32)
    f32, b16 = jnp.float32, jnp.bfloat16
    vmem = pl.BlockSpec(memory_space=pltpu.VMEM)
    smem = pl.BlockSpec(memory_space=pltpu.SMEM)
    hbm = pl.BlockSpec(memory_space=pltpu.HBM)
    rows = pltpu.VMEM((4, depth, lateral), f32)
    eta_rows = pltpu.VMEM((depth, lateral), f32)
    cells = (depth, width, lateral)
    sems = pltpu.SemaphoreType.DMA
    along_y = jnp.asarray(ty)
    result, waves = pl.pallas_call(
        functools.partial(kernel, groups, layers),
        out_shape=(
            pltpu.VMEM((4,) + cells, f32),
            pltpu.VMEM((width, 2 * HALF_MODES), f32),
        ),
        in_specs=[smem, smem] + [hbm] * 6,
        out_specs=(vmem, vmem),
        scratch_shapes=[
            pltpu.VMEM(cells, jnp.int32),
            pltpu.VMEM((4, depth + 2, width, lateral), f32),
            pltpu.VMEM((depth + 2, width, lateral), f32),
            pltpu.VMEM((4, depth + 2, width, lateral), f32),
            pltpu.VMEM(cells, f32),
            pltpu.VMEM(cells, f32),
            rows, rows, rows, rows, rows, rows, rows, rows,
            eta_rows, eta_rows, eta_rows, eta_rows,
            pltpu.VMEM(ty.shape, b16),
            pltpu.VMEM(along_x.shape, b16),
            pltpu.VMEM(bx.shape, b16),
            pltpu.VMEM(cells, f32),
            pltpu.VMEM((layers, 2, groups, width, held), f32),
            shares, shares,
            pltpu.VMEM((groups, 2, width, held), f32),
            pltpu.VMEM((layers, 2, width, held), f32),
            sems((6,)), sems((6,)), sems((24,)), sems((8,)),
            sems((groups,)), sems((groups,)),
        ],
        compiler_params=pltpu.CompilerParams(
            collective_id=0, has_side_effects=True, vmem_limit_bytes=56 * 1024 * 1024
        ),
    )(
        density_table, viscosity_table, phases, velocity, pressure,
        along_y, jnp.asarray(along_x), jnp.asarray(bx),
    )
    return pl.pallas_call(
        last_kernel,
        out_shape=(
            jax.ShapeDtypeStruct(velocity.shape, f32),
            jax.ShapeDtypeStruct(pressure.shape, f32),
            jax.ShapeDtypeStruct((width, lateral), f32),
        ),
        in_specs=[vmem] * 3,
        out_specs=(hbm, hbm, vmem),
        scratch_shapes=[sems((2,))],
        compiler_params=pltpu.CompilerParams(vmem_limit_bytes=16 * 1024 * 1024),
    )(result, waves, along_y)


def local_program(phases, velocity, pressure, density_table, viscosity_table):
    depth, width, lateral = pressure.shape
    groups, layers = lax.axis_size("gx"), lax.axis_size("gz")
    fits = layers == 2 and groups * width == 128 and width == 16 and depth % 8 == 0
    chosen = fused_body if fits else body
    return chosen(phases, velocity, pressure, density_table, viscosity_table)


def solution(mesh):
    in_specs = (
        P(("models", "gz"), "gx", None),
        P(None, ("models", "gz"), "gx", None),
        P(("models", "gz"), "gx", None),
        P(),
        P(),
    )
    out_specs = (
        P(None, ("models", "gz"), "gx", None),
        P(("models", "gz"), "gx", None),
        P(("models", "gx"), None),
    )
    return jax.shard_map(local_program, mesh=mesh, in_specs=in_specs, out_specs=out_specs, check_vma=False)
```
